32 devices in a mesh: groups: 2 (over x), feat: 4 (over y, core), sub: 4 (over z).
Axes of the slice: x: 2, y: 2, z: 4, core: 2. Of those that a mesh axis runs over, the one named last changes fastest.
Arguments:
- hidden: bfloat16 [32, 8192], P('groups', 'feat'), parts along dimension 0, may hold values from -400 to 400
- input_norm_gain: bfloat16 [8192], P('feat'), may hold values from 0.25 to 1.75
- query_weight: bfloat16 [8192, 4096], P('feat', 'sub'), may hold values from -1 to 1
- key_weight: bfloat16 [8192, 512], P('feat', 'sub'), may hold values from -1 to 1
- value_weight: bfloat16 [8192, 512], P('feat', 'sub'), may hold values from -0.0625 to 0.0625
- adapter_down_weight: bfloat16 [8192, 512], P('feat'), may hold values from -0.0625 to 0.0625
- adapter_up_weight: bfloat16 [512, 4096], P(None, 'sub'), may hold values from -0.75 to 0.75
- output_weight: bfloat16 [4096, 8192], P('sub', 'feat'), may hold values from -0.09375 to 0.09375
- request_adapter: int32 [8], P('groups'), parts along dimension 0, may hold values from 0 to 7
- stored_owner: int32 [8, 4], P('groups'), parts along dimension 0, may hold values from 0 to 3, as said below
- stored_lengths: int32 [8], P('groups'), parts along dimension 0, may hold values from 2048 to 8192, as said below
- stored_keys: bfloat16 [16, 8192, 512], P(('groups', 'feat'), None, 'sub'), parts along dimension 0, may hold values from -400 to 400
- stored_values: bfloat16 [16, 8192, 512], P(('groups', 'feat'), None, 'sub'), parts along dimension 0, may hold values from -12 to 12
Outputs:
- attn_out: bfloat16 [32, 8192], P(('groups', 'sub'), 'feat'), parts along dimension 0
The draws below stay inside these ranges and needn't reach their ends.
There are 2 independent parts, one for each index of `groups`. The reference program is written for one: setup_inputs(seed, part) draws one part's arguments, and reference() takes and returns one part's arrays. A program takes and returns all parts, laid end to end along the dimension named above; an argument that names none is the same for every part. Nothing has to cross between parts.
Inputs may be any that keep to these rules, and one draw needn't show every extreme that they name: `stored_owner`: for every key-value head no owner holds more than 2 requests, and some owner holds exactly 2. `stored_lengths`: some request has exactly 8192 cached tokens and some exactly 2048.
All inputs are finite; a program needn't handle non-finite values.
Results may differ from the reference program's by a relative error of at most 0.014.
Values may be sent and summed in bfloat16 or wider, within the bound.
A program may use at most 64 MiB of HBM per device.

```python
import jax
import jax.numpy as jnp
from jax import lax

MODEL_WIDTH = 8192
HEAD_SIZE = 128
GROUP = 8
ADAPTER_RANK = 64
USER_ADAPTERS = 8
REQ_DEV = 1
DRAFT = 4
CTX = 8192
KVH = 4
QUERY_HEADS = 32
REQS = 4
SLOTS = 2
TOKENS = 16
N_FEAT = 4


def draw_hidden(key, part):
    key_a = jax.random.fold_in(jax.random.fold_in(key, 11), 0)
    column = jnp.arange(MODEL_WIDTH, dtype=jnp.float32) / MODEL_WIDTH
    falling = 1.0 - column
    values = jax.random.normal(key_a, (TOKENS, MODEL_WIDTH)) * (3.0 ** falling)[None, :]
    return jnp.clip(values, -400.0, 400.0).astype(jnp.bfloat16)


def head_columns(key, head):
    head_key = jax.random.fold_in(jax.random.fold_in(key, 61), head)
    return jax.random.normal(head_key, (MODEL_WIDTH, HEAD_SIZE)) * MODEL_WIDTH ** (-0.5)


def draw_query_weight(key, part):
    blocks = jax.vmap(lambda head: head_columns(key, head))(jnp.arange(QUERY_HEADS))
    whole = jnp.transpose(blocks, (1, 0, 2)).reshape(MODEL_WIDTH, QUERY_HEADS * HEAD_SIZE)
    return jnp.clip(whole, -1.0, 1.0).astype(jnp.bfloat16)


def draw_key_weight(key, part):
    blocks = jax.vmap(lambda head: head_columns(key, head * GROUP))(jnp.arange(KVH))
    noise = jax.random.normal(jax.random.fold_in(key, 67), (KVH, MODEL_WIDTH, HEAD_SIZE)) * (0.5 * MODEL_WIDTH ** (-0.5))
    whole = jnp.transpose(blocks + noise, (1, 0, 2)).reshape(MODEL_WIDTH, KVH * HEAD_SIZE)
    return jnp.clip(whole, -1.0, 1.0).astype(jnp.bfloat16)


def owner_head(key):
    key_a, key_b, key_c = jax.random.split(key, 3)
    pool = 2 * REQS
    score = jax.random.permutation(key_a, pool).astype(jnp.int32)
    full_owner = jax.random.randint(key_b, (), 0, REQS // REQ_DEV)
    position = jnp.arange(pool)
    score = score - pool * (position // SLOTS == full_owner).astype(jnp.int32)
    chosen = jnp.argsort(score, stable=True)[:REQS]
    chosen = chosen[jax.random.permutation(key_c, REQS)]
    return (chosen // SLOTS).astype(jnp.int32)


def draw_stored_owner(key, part):
    base = jax.random.fold_in(key, 23)
    head_keys = jax.vmap(lambda index: jax.random.fold_in(base, index))(jnp.arange(KVH))
    return jax.vmap(owner_head)(head_keys).T.astype(jnp.int32)


def draw_stored_lengths(key, part):
    key_a, key_b, key_c = jax.random.split(jax.random.fold_in(key, 37), 3)
    values = jax.random.randint(key_a, (REQS,), CTX // 4, CTX + 1)
    longest = jax.random.randint(key_b, (), 0, REQS)
    shortest = (longest + 1 + jax.random.randint(key_c, (), 0, REQS - 1)) % REQS
    index = jnp.arange(REQS)
    values = jnp.where(index == longest, CTX, values)
    values = jnp.where(index == shortest, CTX // 4, values)
    return values.astype(jnp.int32)


def draw_stored_keys(key, part):
    key_a = jax.random.fold_in(jax.random.fold_in(key, 41), 0)
    row_count = N_FEAT * SLOTS
    columns = KVH * HEAD_SIZE
    array_shape = (row_count, CTX, columns)
    values = jax.random.normal(key_a, array_shape)
    return jnp.clip(values, -400.0, 400.0).astype(jnp.bfloat16)


def draw_stored_values(key, part):
    key_a, key_b = jax.random.split(jax.random.fold_in(key, 53), 2)
    array_shape = (N_FEAT * SLOTS, CTX, KVH * HEAD_SIZE)
    offset = jax.random.normal(key_b, (N_FEAT * SLOTS, 1, KVH * HEAD_SIZE))
    values = jax.random.normal(key_a, array_shape) + offset
    return jnp.clip(values, -12.0, 12.0).astype(jnp.bfloat16)


def touch_ends(drawn, rng, low, top_value):
    longest = drawn.shape.index(max(drawn.shape))
    spots = []
    for shift in (0, 1):
        where = [jax.random.randint(jax.random.fold_in(rng, axis), (), 0, length) for axis, length in enumerate(drawn.shape)]
        where[longest] = (where[longest] + shift) % drawn.shape[longest]
        spots.append(tuple(where))
    return drawn.at[spots[0]].set(low).at[spots[1]].set(top_value)


def block_levels(key, shape, cuts, low, high):
    def one(axis_at, shards_of):
        draws = jax.random.uniform(jax.random.fold_in(jax.random.fold_in(key, 6), axis_at), (shards_of,), jnp.float32, low / len(cuts), high / len(cuts))
        return jnp.repeat(jnp.exp(draws), shape[axis_at] // shards_of).reshape((-1,) + (1,) * (len(shape) - axis_at - 1))

    loudness = one(*cuts[0])
    for cut in cuts[1:]:
        loudness = loudness * one(*cut)
    return loudness


def gaussian(own_key, extent, deviation, limit, cuts=(), held_as=jnp.bfloat16):
    drawn = jax.random.normal(own_key, extent, jnp.float32) * deviation
    if len(cuts) > 0:
        drawn = block_levels(own_key, extent, cuts, -0.22, 0.18) * drawn
    return jnp.clip(drawn, min=-limit, max=limit).astype(held_as)


def setup_inputs(seed: int = 0, part: int = 0) -> dict:
    keys = jax.random.split(jax.random.key(seed), 14)
    part_keys = jax.random.split(jax.random.fold_in(keys[13], part), 14)
    hidden = draw_hidden(jax.random.fold_in(jax.random.fold_in(keys[13], part), 71), part)
    input_norm_gain = jnp.clip(1.0 + 0.15 * jax.random.normal(keys[1], (MODEL_WIDTH,), jnp.float32), 0.25, 1.75).astype(jnp.bfloat16)
    query_weight = draw_query_weight(jax.random.fold_in(keys[13], 71), part)
    key_weight = draw_key_weight(jax.random.fold_in(keys[13], 71), part)
    value_weight = gaussian(keys[4], (MODEL_WIDTH, KVH * HEAD_SIZE), MODEL_WIDTH ** -0.5, 0.0625, ((0, 4), (1, 4)))
    adapter_down_weight = gaussian(keys[5], (MODEL_WIDTH, USER_ADAPTERS * ADAPTER_RANK), MODEL_WIDTH ** -0.5, 0.0625, ((0, 4),))
    adapter_up_weight = gaussian(keys[6], (USER_ADAPTERS * ADAPTER_RANK, QUERY_HEADS * HEAD_SIZE), ADAPTER_RANK ** -0.5, 0.75, ((1, 4),))
    output_weight = gaussian(keys[7], (QUERY_HEADS * HEAD_SIZE, MODEL_WIDTH), (QUERY_HEADS * HEAD_SIZE) ** -0.5, 0.09375, ((0, 4), (1, 4)))
    request_adapter = touch_ends(jax.random.randint(part_keys[8], (REQS,), 0, USER_ADAPTERS), jax.random.fold_in(part_keys[8], 1), 0, USER_ADAPTERS - 1).astype(jnp.int32)
    stored_owner = draw_stored_owner(jax.random.fold_in(jax.random.fold_in(keys[13], part), 71), part)
    stored_lengths = draw_stored_lengths(jax.random.fold_in(jax.random.fold_in(keys[13], part), 71), part)
    stored_keys = draw_stored_keys(jax.random.fold_in(jax.random.fold_in(keys[13], part), 71), part)
    stored_values = draw_stored_values(jax.random.fold_in(jax.random.fold_in(keys[13], part), 71), part)
    return {"hidden": hidden, "input_norm_gain": input_norm_gain, "query_weight": query_weight, "key_weight": key_weight, "value_weight": value_weight, "adapter_down_weight": adapter_down_weight, "adapter_up_weight": adapter_up_weight, "output_weight": output_weight, "request_adapter": request_adapter, "stored_owner": stored_owner, "stored_lengths": stored_lengths, "stored_keys": stored_keys, "stored_values": stored_values}


norm_eps = 1e-05
rope_base = 500000.0

def rotate(values, positions):
    half_dim = values.shape[-1] // 2
    inv_freq = rope_base ** (-(jnp.arange(half_dim, dtype=jnp.float32) * 2.0) / values.shape[-1])
    angles = positions * inv_freq
    cosine = jnp.cos(angles)
    sine = jnp.sin(angles)
    first_half = values[..., :half_dim]
    second_half = values[..., half_dim:]
    return jnp.concatenate([first_half * cosine - second_half * sine, second_half * cosine + first_half * sine], axis=-1)

def slot_rows(stored_owner):
    req_iota = jnp.arange(REQS)
    earlier = req_iota[None, :] < req_iota[:, None]
    same_owner = stored_owner[None, :, :] == stored_owner[:, None, :]
    slot_index = lax.optimization_barrier(jnp.sum(jnp.logical_and(same_owner, earlier[:, :, None]).astype(jnp.int32), axis=1))
    return (stored_owner * SLOTS + slot_index).astype(jnp.int32)

def reference(hidden, input_norm_gain, query_weight, key_weight, value_weight, adapter_down_weight, adapter_up_weight, output_weight, request_adapter, stored_owner, stored_lengths, stored_keys, stored_values):
    hidden32 = hidden.astype(jnp.float32)
    mean_square = lax.optimization_barrier(jnp.mean(hidden32 * hidden32, axis=1, keepdims=True))
    normalized_hidden = (hidden32 * lax.rsqrt(mean_square + norm_eps) * input_norm_gain.astype(jnp.float32)).astype(jnp.bfloat16)
    query_unrotated = jnp.dot(normalized_hidden, query_weight, preferred_element_type=jnp.float32)
    key_pre = jnp.dot(normalized_hidden, key_weight, preferred_element_type=jnp.float32)
    value_pre = jnp.dot(normalized_hidden, value_weight, preferred_element_type=jnp.float32)
    tok_adapter = jnp.repeat(request_adapter, DRAFT)
    column_adapter = jnp.arange(USER_ADAPTERS * ADAPTER_RANK) // ADAPTER_RANK
    retain_mask = column_adapter[None, :] == tok_adapter[:, None]
    adapter_middle = jnp.where(retain_mask, jnp.dot(normalized_hidden, adapter_down_weight, preferred_element_type=jnp.float32), 0.0)
    query_unrotated = query_unrotated + jnp.dot(adapter_middle, adapter_up_weight.astype(jnp.float32), precision=lax.Precision.HIGHEST)
    positions = (jnp.repeat(stored_lengths, DRAFT) + jnp.tile(jnp.arange(DRAFT), REQS)).astype(jnp.float32)
    query = rotate(query_unrotated.reshape(TOKENS, QUERY_HEADS, HEAD_SIZE), positions[:, None, None]).astype(jnp.bfloat16)
    key_new = rotate(key_pre.reshape(TOKENS, KVH, HEAD_SIZE), positions[:, None, None]).astype(jnp.bfloat16)
    value_new = value_pre.reshape(TOKENS, KVH, HEAD_SIZE).astype(jnp.bfloat16)
    rows = slot_rows(stored_owner)
    keys_four = stored_keys.reshape(N_FEAT * SLOTS, CTX, KVH, HEAD_SIZE)
    values_four = stored_values.reshape(N_FEAT * SLOTS, CTX, KVH, HEAD_SIZE)
    head_iota = jnp.arange(KVH)
    score_scale = HEAD_SIZE ** (-0.5)
    draft_iota = jnp.arange(DRAFT)
    causal = draft_iota[None, :] <= draft_iota[:, None]

    def request_attention(request):
        start_row = (request * DRAFT).astype(jnp.int32)
        req_query = lax.dynamic_slice_in_dim(query, start_row, DRAFT, 0).reshape(DRAFT, KVH, GROUP, HEAD_SIZE).astype(jnp.float32)
        req_key = lax.dynamic_slice_in_dim(key_new, start_row, DRAFT, 0).astype(jnp.float32)
        req_value = lax.dynamic_slice_in_dim(value_new, start_row, DRAFT, 0).astype(jnp.float32)
        row_here = rows[request]
        old_keys = keys_four[row_here, :, head_iota].astype(jnp.float32)
        old_values = values_four[row_here, :, head_iota].astype(jnp.float32)
        length = stored_lengths[request]
        cache_scores = jnp.einsum('dhgx,hcx->hdgc', req_query, old_keys) * score_scale
        cache_scores = jnp.where(jnp.arange(CTX)[None, None, None, :] < length, cache_scores, -1e+30)
        new_scores = jnp.einsum('dhgx,ehx->hdge', req_query, req_key) * score_scale
        new_scores = jnp.where(causal[None, :, None, :], new_scores, -1e+30)
        row_max = jnp.maximum(lax.optimization_barrier(jnp.max(cache_scores, axis=-1)), lax.optimization_barrier(jnp.max(new_scores, axis=-1)))
        cache_exp = jnp.exp(cache_scores - row_max[..., None])
        new_exp = jnp.exp(new_scores - row_max[..., None])
        total = lax.optimization_barrier(jnp.sum(cache_exp, axis=-1)) + lax.optimization_barrier(jnp.sum(new_exp, axis=-1))
        cache_weights = cache_exp.astype(jnp.bfloat16).astype(jnp.float32)
        new_weights = new_exp.astype(jnp.bfloat16).astype(jnp.float32)
        summed = jnp.einsum('hdgc,hcx->hdgx', cache_weights, old_values) + jnp.einsum('hdge,ehx->hdgx', new_weights, req_value)
        attended = (summed / total[..., None]).astype(jnp.bfloat16)
        return jnp.transpose(attended, (1, 0, 2, 3)).reshape(DRAFT, QUERY_HEADS * HEAD_SIZE)
    attended = lax.map(request_attention, jnp.arange(REQS)).reshape(TOKENS, QUERY_HEADS * HEAD_SIZE)
    return jnp.dot(attended, output_weight, preferred_element_type=jnp.float32).astype(jnp.bfloat16)
```

```python
import functools

import jax
import jax.numpy as jnp
import numpy as np
from jax import lax
from jax.experimental import pallas as pl
from jax.experimental.pallas import tpu as pltpu
from jax.sharding import PartitionSpec as P

ADAPTER_RANK = 64
DRAFT = 4
LANES = 128
SUB16 = 16

norm_eps = 1e-05
rope_base = 500000.0
LOG2E = 1.4426950408889634


def log2(n):
    assert n & (n - 1) == 0
    return n.bit_length() - 1


def wrap(value, n):
    return jnp.where(value >= n, value - n, value)


def kernel(
    feat,
    sub,
    chunk,
    adapter_ref,
    owner_ref,
    length_ref,
    hidden_hbm,
    gain_hbm,
    freq_hbm,
    wq_hbm,
    wk_hbm,
    wv_hbm,
    down_hbm,
    up_hbm,
    wo_hbm,
    keys_hbm,
    values_hbm,
    out_ref,
    hidden,
    gain,
    freq,
    wq,
    wk,
    wv,
    down,
    up,
    wo,
    keys,
    values,
    send_a,
    recv_a,
    send_q,
    recv_q,
    q_stage,
    scores,
    att_stage,
    att_all,
    out_stage,
    send_o,
    recv_o,
    load_sem,
    send_sem,
    recv_sem,
    att_send_sem,
    att_recv_sem,
    out_send_sem,
    out_recv_sem,
):
    f32, bf16, i32 = jnp.float32, jnp.bfloat16, jnp.int32
    me = lax.axis_index("feat")
    my_sub = lax.axis_index("sub")
    tokens, width = hidden.shape
    requests = tokens // DRAFT
    slots, context, head = keys.shape
    rows = slots * DRAFT
    query_cols = wq.shape[1]
    group = query_cols // head
    q_parts = send_q.shape[0]
    q_width = query_cols // q_parts
    lora_cols = down.shape[1]
    d_bits, r_bits, s_bits = log2(DRAFT), log2(rows), log2(slots)
    rank_bits = log2(ADAPTER_RANK)
    halves = SUB16 // rows
    half_cols = query_cols // halves
    out_rows = tokens // sub
    pieces = SUB16 // out_rows
    piece_cols = wo.shape[1] // pieces

    barrier = pltpu.get_barrier_semaphore()
    for o in range(1, feat):
        pl.semaphore_signal(
            barrier, inc=1, device_id={"feat": wrap(me + o, feat)},
            device_id_type=pl.DeviceIdType.MESH,
        )
    for o in range(1, sub):
        pl.semaphore_signal(
            barrier, inc=1, device_id={"sub": wrap(my_sub + o, sub)},
            device_id_type=pl.DeviceIdType.MESH,
        )

    loads = []

    def load(src, dst):
        copy = pltpu.make_async_copy(src, dst, load_sem.at[len(loads)])
        loads.append(copy)
        copy.start()
        return copy

    ld_hidden = load(hidden_hbm, hidden)
    ld_gain = load(gain_hbm, gain)
    ld_freq = load(freq_hbm, freq)
    ld_down = load(down_hbm, down)
    ld_wk = load(wk_hbm, wk)
    ld_wv = load(wv_hbm, wv)
    ld_q = [
        load(wq_hbm.at[:, pl.ds(i * q_width, q_width)], wq.at[:, pl.ds(i * q_width, q_width)])
        for i in range(q_parts)
    ]

    owner = [owner_ref[r, my_sub] for r in range(requests)]
    row_of = []
    for r in range(requests):
        slot = jnp.int32(0)
        for before in range(r):
            slot = slot + jnp.where(owner[before] == owner[r], 1, 0)
        row_of.append(owner[r] * slots + slot)
    adapter = [adapter_ref[r] for r in range(requests)]
    length = [length_ref[r] for r in range(requests)]
    my_adapter, my_length = [], []
    for k in range(slots):
        a, n = jnp.int32(-1), jnp.int32(0)
        for r in range(requests):
            here = row_of[r] == me * slots + k
            a = jnp.where(here, adapter[r], a)
            n = jnp.where(here, length[r], n)
        my_adapter.append(a)
        my_length.append(n)

    def iota(shape, dim):
        return lax.broadcasted_iota(i32, shape, dim)

    def per_request(index, scalars):
        out = jnp.full(index.shape, -1, i32)
        for r in range(requests):
            out = jnp.where(index == r, scalars[r], out)
        return out

    def target_row(j):
        return wrap(me + (j >> r_bits), feat) * slots + ((j >> d_bits) & (slots - 1))

    all_rows = feat * rows
    shape = (all_rows, tokens)
    j, t = iota(shape, 0), iota(shape, 1)
    picked = (per_request(t >> d_bits, row_of) == target_row(j)) & (
        (j & (DRAFT - 1)) == (t & (DRAFT - 1))
    )
    picks = jnp.where(picked, 1.0, 0.0).astype(bf16)

    shape = (all_rows, lora_cols)
    target = target_row(iota(shape, 0))
    row_adapter = jnp.full(shape, -1, i32)
    for r in range(requests):
        row_adapter = jnp.where(target == row_of[r], adapter[r], row_adapter)
    lora_mask = (iota(shape, 1) >> rank_bits) == row_adapter

    def slot_value(shape, scalars):
        index = iota(shape, 0) >> d_bits
        out = jnp.full(shape, scalars[0], i32)
        for k in range(1, slots):
            out = jnp.where(index == k, scalars[k], out)
        return out

    shape = (rows, lora_cols)
    my_lora_mask = (iota(shape, 1) >> rank_bits) == slot_value(shape, my_adapter)

    ld_hidden.wait()
    ld_gain.wait()
    ld_freq.wait()
    picked_hidden = jnp.dot(picks, hidden[...], preferred_element_type=f32)
    x = (picked_hidden * gain[...]).astype(bf16)
    squares = jnp.sum(picked_hidden * picked_hidden, axis=1, keepdims=True)

    shape = (rows, head)
    position = (slot_value(shape, my_length) + (iota(shape, 0) & (DRAFT - 1))).astype(f32)
    angle = position * freq[...]
    cosine = jnp.cos(angle)
    sine = jnp.sin(angle)
    sine = jnp.where(iota(shape, 1) < head // 2, -sine, sine)

    sends = []

    def send(src, dst, ssem, rsem, device):
        copy = pltpu.make_async_remote_copy(
            src_ref=src, dst_ref=dst, send_sem=ssem, recv_sem=rsem,
            device_id=device, device_id_type=pl.DeviceIdType.MESH,
        )
        copy.start()
        sends.append(copy)
        return copy

    ld_wk.wait()
    ld_wv.wait()
    ld_down.wait()
    ld_k = [load(keys_hbm.at[s], keys.at[s]) for s in range(slots)]
    ld_up = load(up_hbm, up)
    part_k = jnp.dot(x, wk[...], preferred_element_type=f32)
    part_v = jnp.dot(x, wv[...], preferred_element_type=f32)
    lora = jnp.where(lora_mask, jnp.dot(x, down[...], preferred_element_type=f32), 0.0)
    folded = lora[:, :LANES]
    for i in range(1, lora_cols // LANES):
        folded = folded + lora[:, i * LANES : (i + 1) * LANES]
    send_a[:, 0:head] = part_k
    send_a[:, head : 2 * head] = part_v
    send_a[:, 2 * head : 2 * head + LANES] = folded
    send_a[:, 2 * head + LANES :] = jnp.broadcast_to(squares, (all_rows, LANES))
    pl.semaphore_wait(barrier, feat + sub - 2)
    first = []
    for o in range(1, feat):
        block = pl.ds(o * rows, rows)
        first.append(
            send(
                send_a.at[block], recv_a.at[block], send_sem.at[0, o], recv_sem.at[0, o],
                {"feat": wrap(me + o, feat)},
            )
        )
    ld_v = []
    for i in range(q_parts):
        ld_q[i].wait()
        if i == 0:
            ld_v = [load(values_hbm.at[s], values.at[s]) for s in range(slots)]
        if i == q_parts - 1:
            ld_o = load(wo_hbm, wo)
        send_q[i] = jnp.dot(
            x, wq[:, i * q_width : (i + 1) * q_width], preferred_element_type=f32
        )
        for o in range(1, feat):
            block = pl.ds(o * rows, rows)
            first.append(
                send(
                    send_q.at[i, block], recv_q.at[i, block],
                    send_sem.at[1 + i, o], recv_sem.at[1 + i, o],
                    {"feat": wrap(me + o, feat)},
                )
            )
    ld_up.wait()
    for copy in first[: feat - 1]:
        copy.wait_recv()
    total_a = send_a[0:rows]
    for o in range(1, feat):
        total_a = total_a + recv_a[o * rows : (o + 1) * rows]
    scale = lax.rsqrt(total_a[:, 2 * head + LANES :] / (width * feat) + norm_eps)
    mid = total_a[:, 2 * head : 2 * head + LANES]
    mid = jnp.where(my_lora_mask, jnp.concatenate([mid] * (lora_cols // LANES), axis=1), 0.0)
    mid1 = mid.astype(bf16).astype(f32)
    rest = mid - mid1
    mid2 = rest.astype(bf16).astype(f32)
    mid3 = rest - mid2
    stacked = jnp.concatenate([mid1, mid2, mid3, jnp.zeros_like(mid)], axis=0).astype(bf16)
    lifted = jnp.dot(stacked, up[...], preferred_element_type=f32)
    lifted = lifted[0:rows] + lifted[rows : 2 * rows] + lifted[2 * rows : 3 * rows]

    def rotate(values_in):
        return values_in * cosine + pltpu.roll(values_in, head // 2, 1) * sine

    key_new = rotate(total_a[:, 0:head] * scale)
    value_new = total_a[:, head : 2 * head] * scale
    filler = jnp.zeros((LANES - rows, head), f32)
    key_new = jnp.concatenate([key_new, filler], axis=0).astype(bf16)
    value_new = jnp.concatenate([value_new, filler], axis=0).astype(bf16)

    for copy in first[feat - 1 :]:
        copy.wait_recv()
    for i in range(q_parts):
        total_q = send_q[i, 0:rows]
        for o in range(1, feat):
            total_q = total_q + recv_q[i, o * rows : (o + 1) * rows]
        for g in range(q_width // head):
            whole_g = i * (q_width // head) + g
            part = total_q[:, g * head : (g + 1) * head]
            part = part + lifted[:, whole_g * head : (whole_g + 1) * head]
            part = rotate(part * scale)
            for s in range(slots):
                q_stage[s, whole_g * DRAFT : (whole_g + 1) * DRAFT, :] = part[
                    s * DRAFT : (s + 1) * DRAFT
                ]

    for copy in ld_k + ld_v:
        copy.wait()
    factor = head ** (-0.5) * LOG2E
    q_rows = group * DRAFT
    chunks = context // chunk
    contract = (((1,), (1,)), ((), ()))
    shape = (q_rows, LANES)
    lane, row_d = iota(shape, 1), iota(shape, 0) & (DRAFT - 1)
    queries = [q_stage[s].astype(bf16) for s in range(slots)]
    new_scores, row_max = [], []
    for s in range(slots):
        fresh = lax.dot_general(queries[s], key_new, contract, preferred_element_type=f32)
        seen = (lane >= s * DRAFT) & (lane - s * DRAFT <= row_d)
        fresh = jnp.where(seen, fresh, -1e30)
        new_scores.append(fresh)
        top = fresh
        for c in range(chunks):
            block = lax.dot_general(
                queries[s], keys[s, c * chunk : (c + 1) * chunk, :], contract,
                preferred_element_type=f32,
            )
            valid = iota((q_rows, chunk), 1) < my_length[s] - c * chunk
            block = jnp.where(valid, block, -1e30)
            scores[s, :, c * chunk : (c + 1) * chunk] = block
            for i in range(chunk // LANES):
                top = jnp.maximum(top, block[:, i * LANES : (i + 1) * LANES])
        row_max.append(jnp.max(top, axis=1, keepdims=True))
    for s in range(slots):
        weights = jnp.exp2((new_scores[s] - row_max[s]) * factor)
        total = weights
        summed = jnp.dot(weights.astype(bf16), value_new, preferred_element_type=f32)
        for c in range(chunks):
            weights = jnp.exp2(
                (scores[s, :, c * chunk : (c + 1) * chunk] - row_max[s]) * factor
            )
            for i in range(chunk // LANES):
                total = total + weights[:, i * LANES : (i + 1) * LANES]
            summed = summed + jnp.dot(
                weights.astype(bf16), values[s, c * chunk : (c + 1) * chunk, :],
                preferred_element_type=f32,
            )
        attended = summed / jnp.sum(total, axis=1, keepdims=True)
        per_half = group // halves
        for g in range(group):
            h, at = g // per_half, g % per_half
            first_row = h * rows + s * DRAFT
            att_stage[first_row : first_row + DRAFT, at * head : (at + 1) * head] = attended[
                g * DRAFT : (g + 1) * DRAFT
            ]
    att_all[0:SUB16, :] = att_stage[...].astype(bf16)
    second = []
    for o in range(1, feat):
        second.append(
            send(
                att_all.at[pl.ds(0, SUB16)], att_all.at[pl.ds(o * SUB16, SUB16)],
                att_send_sem.at[o], att_recv_sem.at[o], {"feat": wrap(me + o, feat)},
            )
        )
    shape = (tokens, feat * SUB16)
    t, jj = iota(shape, 0), iota(shape, 1)
    out_bits = log2(out_rows)
    token = (wrap(my_sub + (t >> out_bits), sub) << out_bits) + (t & (out_rows - 1))
    source = me - (jj >> log2(SUB16))
    source = jnp.where(source < 0, source + feat, source)
    wanted = source * slots + ((jj >> d_bits) & (slots - 1))
    match = (per_request(token >> d_bits, row_of) == wanted) & (
        (token & (DRAFT - 1)) == (jj & (DRAFT - 1))
    )
    in_half = (jj & (SUB16 - 1)) >> r_bits
    ld_o.wait()
    for copy in second:
        copy.wait_recv()
    token_rows = jnp.concatenate(
        [
            jnp.dot(
                jnp.where(match & (in_half == h), 1.0, 0.0).astype(bf16), att_all[...],
                preferred_element_type=f32,
            )
            for h in range(halves)
        ],
        axis=1,
    ).astype(bf16)
    for p in range(pieces):
        block = jnp.dot(
            token_rows, wo[:, p * piece_cols : (p + 1) * piece_cols], preferred_element_type=f32
        )
        for o in range(sub):
            out_stage[o, p * out_rows : (p + 1) * out_rows, :] = block[
                o * out_rows : (o + 1) * out_rows
            ]
    third = []
    for o in range(1, sub):
        send_o[o] = out_stage[o].astype(bf16)
        third.append(
            send(
                send_o.at[o], recv_o.at[o], out_send_sem.at[o], out_recv_sem.at[o],
                {"sub": wrap(my_sub + o, sub)},
            )
        )
    for copy in third:
        copy.wait_recv()
    result = out_stage[0]
    for o in range(1, sub):
        result = result + recv_o[o].astype(f32)
    for p in range(pieces):
        out_ref[:, p * piece_cols : (p + 1) * piece_cols] = result[
            p * out_rows : (p + 1) * out_rows
        ].astype(bf16)
    for copy in sends:
        copy.wait_send()


def body(
    hidden,
    input_norm_gain,
    query_weight,
    key_weight,
    value_weight,
    adapter_down_weight,
    adapter_up_weight,
    output_weight,
    request_adapter,
    stored_owner,
    stored_lengths,
    stored_keys,
    stored_values,
):
    f32, bf16 = jnp.float32, jnp.bfloat16
    feat = lax.axis_size("feat")
    sub = lax.axis_size("sub")
    tokens, width = hidden.shape
    slots, context, head = stored_keys.shape
    rows = slots * DRAFT
    query_cols = query_weight.shape[1]
    out_cols = output_weight.shape[1]
    out_rows = tokens // sub
    q_parts = 2
    chunk = min(2048, context)
    pieces = SUB16 // out_rows
    half = head // 2
    inv_freq = (rope_base ** (-(np.arange(half) * 2.0) / head)).astype(np.float32)
    freq = jnp.asarray(np.tile(np.concatenate([inv_freq, inv_freq])[None, :], (rows, 1)))
    gain = input_norm_gain.astype(f32)[None, :]
    any_spec = pl.BlockSpec(memory_space=pl.ANY)
    smem = pl.BlockSpec(memory_space=pltpu.SMEM)
    V = pltpu.VMEM
    a_cols = 2 * head + 2 * LANES
    scratch = [
        V(hidden.shape, bf16),
        V(gain.shape, f32),
        V(freq.shape, f32),
        V(query_weight.shape, bf16),
        V(key_weight.shape, bf16),
        V(value_weight.shape, bf16),
        V(adapter_down_weight.shape, bf16),
        V(adapter_up_weight.shape, bf16),
        V(output_weight.shape, bf16),
        V(stored_keys.shape, bf16),
        V(stored_values.shape, bf16),
        V((feat * rows, a_cols), f32),
        V((feat * rows, a_cols), f32),
        V((q_parts, feat * rows, query_cols // q_parts), f32),
        V((q_parts, feat * rows, query_cols // q_parts), f32),
        V((slots, query_cols // head * DRAFT, head), f32),
        V((slots, query_cols // head * DRAFT, context), f32),
        V((SUB16, query_cols * rows // SUB16), f32),
        V((feat * SUB16, query_cols * rows // SUB16), bf16),
        V((sub, SUB16, out_cols // pieces), f32),
        V((sub, SUB16, out_cols // pieces), bf16),
        V((sub, SUB16, out_cols // pieces), bf16),
        pltpu.SemaphoreType.DMA((8 + q_parts + 2 * slots,)),
        pltpu.SemaphoreType.DMA((1 + q_parts, feat)),
        pltpu.SemaphoreType.DMA((1 + q_parts, feat)),
        pltpu.SemaphoreType.DMA((feat,)),
        pltpu.SemaphoreType.DMA((feat,)),
        pltpu.SemaphoreType.DMA((sub,)),
        pltpu.SemaphoreType.DMA((sub,)),
    ]
    return pl.pallas_call(
        functools.partial(kernel, feat, sub, chunk),
        out_shape=jax.ShapeDtypeStruct((out_rows, out_cols), bf16),
        in_specs=[smem] * 3 + [any_spec] * 11,
        out_specs=pl.BlockSpec(memory_space=pltpu.VMEM),
        scratch_shapes=scratch,
        compiler_params=pltpu.CompilerParams(
            collective_id=0, has_side_effects=True, vmem_limit_bytes=48 * 1024 * 1024
        ),
    )(
        request_adapter,
        stored_owner,
        stored_lengths,
        hidden,
        gain,
        freq,
        query_weight,
        key_weight,
        value_weight,
        adapter_down_weight,
        adapter_up_weight,
        output_weight,
        stored_keys,
        stored_values,
    )


def solution(mesh):
    in_specs = (
        P("groups", "feat"),
        P("feat"),
        P("feat", "sub"),
        P("feat", "sub"),
        P("feat", "sub"),
        P("feat", None),
        P(None, "sub"),
        P("sub", "feat"),
        P("groups"),
        P("groups", None),
        P("groups"),
        P(("groups", "feat"), None, "sub"),
        P(("groups", "feat"), None, "sub"),
    )
    out_specs = P(("groups", "sub"), "feat")
    return jax.shard_map(body, mesh=mesh, in_specs=in_specs, out_specs=out_specs, check_vma=False)
```

```python
import functools

import jax
import jax.numpy as jnp
import numpy as np
from jax import lax
from jax.experimental import pallas as pl
from jax.experimental.pallas import tpu as pltpu
from jax.sharding import PartitionSpec as P

ADAPTER_RANK = 64
DRAFT = 4
LANES = 128
SUB16 = 16

norm_eps = 1e-05
rope_base = 500000.0
LOG2E = 1.4426950408889634


def log2(n):
    assert n & (n - 1) == 0
    return n.bit_length() - 1


def wrap(value, n):
    return jnp.where(value >= n, value - n, value)


def kernel(
    feat,
    sub,
    chunk,
    adapter_hbm,
    owner_hbm,
    length_hbm,
    hidden_hbm,
    gain_hbm,
    freq_hbm,
    wq_hbm,
    wk_hbm,
    wv_hbm,
    down_hbm,
    up_hbm,
    wo_hbm,
    keys_hbm,
    values_hbm,
    out_ref,
    adapter_ref,
    owner_ref,
    length_ref,
    hidden,
    gain,
    freq,
    wq,
    wk,
    wv,
    down,
    up,
    wo,
    keys,
    values,
    send_a,
    recv_a,
    send_q,
    recv_q,
    q_stage,
    scores,
    att_stage,
    att_all,
    out_stage,
    send_o,
    recv_o,
    load_sem,
    send_sem,
    recv_sem,
    att_send_sem,
    att_recv_sem,
    out_send_sem,
    out_recv_sem,
):
    f32, bf16, i32 = jnp.float32, jnp.bfloat16, jnp.int32
    me = lax.axis_index("feat")
    my_sub = lax.axis_index("sub")
    tokens, width = hidden.shape
    requests = tokens // DRAFT
    slots, context, head = keys.shape
    rows = slots * DRAFT
    query_cols = wq.shape[1]
    group = query_cols // head
    q_parts = send_q.shape[0]
    q_width = query_cols // q_parts
    lora_cols = down.shape[1]
    d_bits, r_bits, s_bits = log2(DRAFT), log2(rows), log2(slots)
    rank_bits = log2(ADAPTER_RANK)
    halves = SUB16 // rows
    half_cols = query_cols // halves
    out_rows = tokens // sub
    pieces = SUB16 // out_rows
    piece_cols = wo.shape[1] // pieces

    barrier = pltpu.get_barrier_semaphore()
    for o in range(1, feat):
        pl.semaphore_signal(
            barrier, inc=1, device_id={"feat": wrap(me + o, feat)},
            device_id_type=pl.DeviceIdType.MESH,
        )
    for o in range(1, sub):
        pl.semaphore_signal(
            barrier, inc=1, device_id={"sub": wrap(my_sub + o, sub)},
            device_id_type=pl.DeviceIdType.MESH,
        )

    loads = []

    def load(src, dst):
        copy = pltpu.make_async_copy(src, dst, load_sem.at[len(loads)])
        loads.append(copy)
        copy.start()
        return copy

    ld_index = [
        load(owner_hbm, owner_ref), load(adapter_hbm, adapter_ref), load(length_hbm, length_ref)
    ]
    ld_hidden = load(hidden_hbm, hidden)
    ld_gain = load(gain_hbm, gain)
    ld_freq = load(freq_hbm, freq)
    ld_down = load(down_hbm, down)
    ld_wk = load(wk_hbm, wk)
    ld_wv = load(wv_hbm, wv)
    ld_q = [
        load(wq_hbm.at[:, pl.ds(i * q_width, q_width)], wq.at[:, pl.ds(i * q_width, q_width)])
        for i in range(q_parts)
    ]

    for copy in ld_index:
        copy.wait()
    owner = [owner_ref[r, my_sub] for r in range(requests)]
    row_of = []
    for r in range(requests):
        slot = jnp.int32(0)
        for before in range(r):
            slot = slot + jnp.where(owner[before] == owner[r], 1, 0)
        row_of.append(owner[r] * slots + slot)
    adapter = [adapter_ref[r] for r in range(requests)]
    length = [length_ref[r] for r in range(requests)]
    my_adapter, my_length = [], []
    for k in range(slots):
        a, n = jnp.int32(-1), jnp.int32(0)
        for r in range(requests):
            here = row_of[r] == me * slots + k
            a = jnp.where(here, adapter[r], a)
            n = jnp.where(here, length[r], n)
        my_adapter.append(a)
        my_length.append(n)

    def iota(shape, dim):
        return lax.broadcasted_iota(i32, shape, dim)

    def per_request(index, scalars):
        out = jnp.full(index.shape, -1, i32)
        for r in range(requests):
            out = jnp.where(index == r, scalars[r], out)
        return out

    def target_row(j):
        return wrap(me + (j >> r_bits), feat) * slots + ((j >> d_bits) & (slots - 1))

    all_rows = feat * rows
    shape = (all_rows, tokens)
    j, t = iota(shape, 0), iota(shape, 1)
    picked = (per_request(t >> d_bits, row_of) == target_row(j)) & (
        (j & (DRAFT - 1)) == (t & (DRAFT - 1))
    )
    picks = jnp.where(picked, 1.0, 0.0).astype(bf16)

    shape = (all_rows, lora_cols)
    target = target_row(iota(shape, 0))
    row_adapter = jnp.full(shape, -1, i32)
    for r in range(requests):
        row_adapter = jnp.where(target == row_of[r], adapter[r], row_adapter)
    lora_mask = (iota(shape, 1) >> rank_bits) == row_adapter

    def slot_value(shape, scalars):
        index = iota(shape, 0) >> d_bits
        out = jnp.full(shape, scalars[0], i32)
        for k in range(1, slots):
            out = jnp.where(index == k, scalars[k], out)
        return out

    shape = (rows, lora_cols)
    my_lora_mask = (iota(shape, 1) >> rank_bits) == slot_value(shape, my_adapter)

    ld_hidden.wait()
    ld_gain.wait()
    ld_freq.wait()
    picked_hidden = jnp.dot(picks, hidden[...], preferred_element_type=f32)
    gains = gain[...].astype(f32)
    x = jnp.concatenate(
        [
            picked_hidden[:, i * LANES : (i + 1) * LANES] * gains[i : i + 1, :]
            for i in range(width // LANES)
        ],
        axis=1,
    ).astype(bf16)
    squares = jnp.sum(picked_hidden * picked_hidden, axis=1, keepdims=True)

    shape = (rows, head)
    position = (slot_value(shape, my_length) + (iota(shape, 0) & (DRAFT - 1))).astype(f32)
    angle = position * freq[...]
    cosine = jnp.cos(angle)
    sine = jnp.sin(angle)
    sine = jnp.where(iota(shape, 1) < head // 2, -sine, sine)

    sends = []

    def send(src, dst, ssem, rsem, device):
        copy = pltpu.make_async_remote_copy(
            src_ref=src, dst_ref=dst, send_sem=ssem, recv_sem=rsem,
            device_id=device, device_id_type=pl.DeviceIdType.MESH,
        )
        copy.start()
        sends.append(copy)
        return copy

    ld_wk.wait()
    ld_wv.wait()
    ld_down.wait()
    ld_k = [load(keys_hbm.at[s], keys.at[s]) for s in range(slots)]
    ld_up = load(up_hbm, up)
    part_k = jnp.dot(x, wk[...], preferred_element_type=f32)
    part_v = jnp.dot(x, wv[...], preferred_element_type=f32)
    lora = jnp.where(lora_mask, jnp.dot(x, down[...], preferred_element_type=f32), 0.0)
    folded = lora[:, :LANES]
    for i in range(1, lora_cols // LANES):
        folded = folded + lora[:, i * LANES : (i + 1) * LANES]
    send_a[:, 0:head] = part_k
    send_a[:, head : 2 * head] = part_v
    send_a[:, 2 * head : 2 * head + LANES] = folded
    send_a[:, 2 * head + LANES :] = jnp.broadcast_to(squares, (all_rows, LANES))
    pl.semaphore_wait(barrier, feat + sub - 2)
    first = []
    for o in range(1, feat):
        block = pl.ds(o * rows, rows)
        first.append(
            send(
                send_a.at[block], recv_a.at[block], send_sem.at[0, o], recv_sem.at[0, o],
                {"feat": wrap(me + o, feat)},
            )
        )
    ld_v = []
    for i in range(q_parts):
        ld_q[i].wait()
        if i == 0:
            ld_v = [load(values_hbm.at[s], values.at[s]) for s in range(slots)]
        if i == q_parts - 1:
            ld_o = load(wo_hbm, wo)
        send_q[i] = jnp.dot(
            x, wq[:, i * q_width : (i + 1) * q_width], preferred_element_type=f32
        )
        for o in range(1, feat):
            block = pl.ds(o * rows, rows)
            first.append(
                send(
                    send_q.at[i, block], recv_q.at[i, block],
                    send_sem.at[1 + i, o], recv_sem.at[1 + i, o],
                    {"feat": wrap(me + o, feat)},
                )
            )
    ld_up.wait()
    for copy in first[: feat - 1]:
        copy.wait_recv()
    total_a = send_a[0:rows]
    for o in range(1, feat):
        total_a = total_a + recv_a[o * rows : (o + 1) * rows]
    scale = lax.rsqrt(total_a[:, 2 * head + LANES :] / (width * feat) + norm_eps)
    mid = total_a[:, 2 * head : 2 * head + LANES]
    mid = jnp.where(my_lora_mask, jnp.concatenate([mid] * (lora_cols // LANES), axis=1), 0.0)
    mid1 = mid.astype(bf16).astype(f32)
    rest = mid - mid1
    mid2 = rest.astype(bf16).astype(f32)
    mid3 = rest - mid2
    stacked = jnp.concatenate([mid1, mid2, mid3, jnp.zeros_like(mid)], axis=0).astype(bf16)
    lifted = jnp.dot(stacked, up[...], preferred_element_type=f32)
    lifted = lifted[0:rows] + lifted[rows : 2 * rows] + lifted[2 * rows : 3 * rows]

    def rotate(values_in):
        return values_in * cosine + pltpu.roll(values_in, head // 2, 1) * sine

    key_new = rotate(total_a[:, 0:head] * scale)
    value_new = total_a[:, head : 2 * head] * scale
    filler = jnp.zeros((LANES - rows, head), f32)
    key_new = jnp.concatenate([key_new, filler], axis=0).astype(bf16)
    value_new = jnp.concatenate([value_new, filler], axis=0).astype(bf16)

    for copy in first[feat - 1 :]:
        copy.wait_recv()
    for i in range(q_parts):
        total_q = send_q[i, 0:rows]
        for o in range(1, feat):
            total_q = total_q + recv_q[i, o * rows : (o + 1) * rows]
        for g in range(q_width // head):
            whole_g = i * (q_width // head) + g
            part = total_q[:, g * head : (g + 1) * head]
            part = part + lifted[:, whole_g * head : (whole_g + 1) * head]
            part = rotate(part * scale)
            for s in range(slots):
                q_stage[s, whole_g * DRAFT : (whole_g + 1) * DRAFT, :] = part[
                    s * DRAFT : (s + 1) * DRAFT
                ]

    for copy in ld_k + ld_v:
        copy.wait()
    factor = head ** (-0.5) * LOG2E
    q_rows = group * DRAFT
    chunks = context // chunk
    contract = (((1,), (1,)), ((), ()))
    shape = (q_rows, LANES)
    lane, row_d = iota(shape, 1), iota(shape, 0) & (DRAFT - 1)
    queries = [q_stage[s].astype(bf16) for s in range(slots)]
    new_scores, row_max = [], []
    for s in range(slots):
        fresh = lax.dot_general(queries[s], key_new, contract, preferred_element_type=f32)
        seen = (lane >= s * DRAFT) & (lane - s * DRAFT <= row_d)
        fresh = jnp.where(seen, fresh, -1e30)
        new_scores.append(fresh)
        top = fresh
        for c in range(chunks):
            block = lax.dot_general(
                queries[s], keys[s, c * chunk : (c + 1) * chunk, :], contract,
                preferred_element_type=f32,
            )
            valid = iota((q_rows, chunk), 1) < my_length[s] - c * chunk
            block = jnp.where(valid, block, -1e30)
            scores[s, :, c * chunk : (c + 1) * chunk] = block
            for i in range(chunk // LANES):
                top = jnp.maximum(top, block[:, i * LANES : (i + 1) * LANES])
        row_max.append(jnp.max(top, axis=1, keepdims=True))
    for s in range(slots):
        weights = jnp.exp2((new_scores[s] - row_max[s]) * factor)
        total = weights
        summed = jnp.dot(weights.astype(bf16), value_new, preferred_element_type=f32)
        for c in range(chunks):
            weights = jnp.exp2(
                (scores[s, :, c * chunk : (c + 1) * chunk] - row_max[s]) * factor
            )
            for i in range(chunk // LANES):
                total = total + weights[:, i * LANES : (i + 1) * LANES]
            summed = summed + jnp.dot(
                weights.astype(bf16), values[s, c * chunk : (c + 1) * chunk, :],
                preferred_element_type=f32,
            )
        attended = summed / jnp.sum(total, axis=1, keepdims=True)
        per_half = group // halves
        for g in range(group):
            h, at = g // per_half, g % per_half
            first_row = h * rows + s * DRAFT
            att_stage[first_row : first_row + DRAFT, at * head : (at + 1) * head] = attended[
                g * DRAFT : (g + 1) * DRAFT
            ]
    att_all[0:SUB16, :] = att_stage[...].astype(bf16)
    second = []
    for o in range(1, feat):
        second.append(
            send(
                att_all.at[pl.ds(0, SUB16)], att_all.at[pl.ds(o * SUB16, SUB16)],
                att_send_sem.at[o], att_recv_sem.at[o], {"feat": wrap(me + o, feat)},
            )
        )
    shape = (tokens, feat * SUB16)
    t, jj = iota(shape, 0), iota(shape, 1)
    out_bits = log2(out_rows)
    token = (wrap(my_sub + (t >> out_bits), sub) << out_bits) + (t & (out_rows - 1))
    source = me - (jj >> log2(SUB16))
    source = jnp.where(source < 0, source + feat, source)
    wanted = source * slots + ((jj >> d_bits) & (slots - 1))
    match = (per_request(token >> d_bits, row_of) == wanted) & (
        (token & (DRAFT - 1)) == (jj & (DRAFT - 1))
    )
    in_half = (jj & (SUB16 - 1)) >> r_bits
    ld_o.wait()
    for copy in second:
        copy.wait_recv()
    token_rows = jnp.concatenate(
        [
            jnp.dot(
                jnp.where(match & (in_half == h), 1.0, 0.0).astype(bf16), att_all[...],
                preferred_element_type=f32,
            )
            for h in range(halves)
        ],
        axis=1,
    ).astype(bf16)
    for p in range(pieces):
        block = jnp.dot(
            token_rows, wo[:, p * piece_cols : (p + 1) * piece_cols], preferred_element_type=f32
        )
        for o in range(sub):
            out_stage[o, p * out_rows : (p + 1) * out_rows, :] = block[
                o * out_rows : (o + 1) * out_rows
            ]
    third = []
    for o in range(1, sub):
        send_o[o] = out_stage[o].astype(bf16)
        third.append(
            send(
                send_o.at[o], recv_o.at[o], out_send_sem.at[o], out_recv_sem.at[o],
                {"sub": wrap(my_sub + o, sub)},
            )
        )
    for copy in third:
        copy.wait_recv()
    result = out_stage[0]
    for o in range(1, sub):
        result = result + recv_o[o].astype(f32)
    for p in range(pieces):
        out_ref[:, p * piece_cols : (p + 1) * piece_cols] = result[
            p * out_rows : (p + 1) * out_rows
        ].astype(bf16)
    for copy in sends:
        copy.wait_send()


def body(
    hidden,
    input_norm_gain,
    query_weight,
    key_weight,
    value_weight,
    adapter_down_weight,
    adapter_up_weight,
    output_weight,
    request_adapter,
    stored_owner,
    stored_lengths,
    stored_keys,
    stored_values,
):
    f32, bf16 = jnp.float32, jnp.bfloat16
    feat = lax.axis_size("feat")
    sub = lax.axis_size("sub")
    tokens, width = hidden.shape
    slots, context, head = stored_keys.shape
    rows = slots * DRAFT
    query_cols = query_weight.shape[1]
    out_cols = output_weight.shape[1]
    out_rows = tokens // sub
    q_parts = 2
    chunk = min(2048, context)
    pieces = SUB16 // out_rows
    half = head // 2
    inv_freq = (rope_base ** (-(np.arange(half) * 2.0) / head)).astype(np.float32)
    freq = jnp.asarray(np.tile(np.concatenate([inv_freq, inv_freq])[None, :], (rows, 1)))
    gain = input_norm_gain.reshape(-1, LANES)
    any_spec = pl.BlockSpec(memory_space=pl.ANY)
    V = pltpu.VMEM
    a_cols = 2 * head + 2 * LANES
    scratch = [
        pltpu.SMEM(request_adapter.shape, jnp.int32),
        pltpu.SMEM(stored_owner.shape, jnp.int32),
        pltpu.SMEM(stored_lengths.shape, jnp.int32),
        V(hidden.shape, bf16),
        V(gain.shape, bf16),
        V(freq.shape, f32),
        V(query_weight.shape, bf16),
        V(key_weight.shape, bf16),
        V(value_weight.shape, bf16),
        V(adapter_down_weight.shape, bf16),
        V(adapter_up_weight.shape, bf16),
        V(output_weight.shape, bf16),
        V(stored_keys.shape, bf16),
        V(stored_values.shape, bf16),
        V((feat * rows, a_cols), f32),
        V((feat * rows, a_cols), f32),
        V((q_parts, feat * rows, query_cols // q_parts), f32),
        V((q_parts, feat * rows, query_cols // q_parts), f32),
        V((slots, query_cols // head * DRAFT, head), f32),
        V((slots, query_cols // head * DRAFT, context), f32),
        V((SUB16, query_cols * rows // SUB16), f32),
        V((feat * SUB16, query_cols * rows // SUB16), bf16),
        V((sub, SUB16, out_cols // pieces), f32),
        V((sub, SUB16, out_cols // pieces), bf16),
        V((sub, SUB16, out_cols // pieces), bf16),
        pltpu.SemaphoreType.DMA((11 + q_parts + 2 * slots,)),
        pltpu.SemaphoreType.DMA((1 + q_parts, feat)),
        pltpu.SemaphoreType.DMA((1 + q_parts, feat)),
        pltpu.SemaphoreType.DMA((feat,)),
        pltpu.SemaphoreType.DMA((feat,)),
        pltpu.SemaphoreType.DMA((sub,)),
        pltpu.SemaphoreType.DMA((sub,)),
    ]
    return pl.pallas_call(
        functools.partial(kernel, feat, sub, chunk),
        out_shape=jax.ShapeDtypeStruct((out_rows, out_cols), bf16),
        in_specs=[any_spec] * 14,
        out_specs=pl.BlockSpec(memory_space=pltpu.VMEM),
        scratch_shapes=scratch,
        compiler_params=pltpu.CompilerParams(
            collective_id=0, has_side_effects=True, vmem_limit_bytes=64 * 1024 * 1024
        ),
    )(
        request_adapter,
        stored_owner,
        stored_lengths,
        hidden,
        gain,
        freq,
        query_weight,
        key_weight,
        value_weight,
        adapter_down_weight,
        adapter_up_weight,
        output_weight,
        stored_keys,
        stored_values,
    )


def solution(mesh):
    in_specs = (
        P("groups", "feat"),
        P("feat"),
        P("feat", "sub"),
        P("feat", "sub"),
        P("feat", "sub"),
        P("feat", None),
        P(None, "sub"),
        P("sub", "feat"),
        P("groups"),
        P("groups", None),
        P("groups"),
        P(("groups", "feat"), None, "sub"),
        P(("groups", "feat"), None, "sub"),
    )
    out_specs = P(("groups", "sub"), "feat")
    return jax.shard_map(body, mesh=mesh, in_specs=in_specs, out_specs=out_specs, check_vma=False)
```

```python
import functools

import jax
import jax.numpy as jnp
import numpy as np
from jax import lax
from jax.experimental import pallas as pl
from jax.experimental.pallas import tpu as pltpu
from jax.sharding import PartitionSpec as P

ADAPTER_RANK = 64
DRAFT = 4
LANES = 128
SUB16 = 16

norm_eps = 1e-05
rope_base = 500000.0
LOG2E = 1.4426950408889634


def log2(n):
    assert n & (n - 1) == 0
    return n.bit_length() - 1


def wrap(value, n):
    return jnp.where(value >= n, value - n, value)


def kernel(
    feat,
    sub,
    chunk,
    adapter_hbm,
    owner_hbm,
    length_hbm,
    hidden_hbm,
    gain_hbm,
    freq_hbm,
    wq_hbm,
    wk_hbm,
    wv_hbm,
    down_hbm,
    up_hbm,
    wo_hbm,
    keys_hbm,
    values_hbm,
    out_ref,
    adapter_ref,
    owner_ref,
    length_ref,
    hidden,
    gain,
    freq,
    wq,
    wk,
    wv,
    down,
    up,
    wo,
    keys,
    values,
    send_a,
    recv_a,
    send_q,
    recv_q,
    q_stage,
    scores,
    att_stage,
    att_all,
    out_stage,
    send_o,
    recv_o,
    load_sem,
    send_sem,
    recv_sem,
    att_send_sem,
    att_recv_sem,
    out_send_sem,
    out_recv_sem,
):
    f32, bf16, i32 = jnp.float32, jnp.bfloat16, jnp.int32
    me = lax.axis_index("feat")
    my_sub = lax.axis_index("sub")
    tokens, width = hidden.shape
    requests = tokens // DRAFT
    slots, context, head = keys_hbm.shape
    rows = slots * DRAFT
    query_cols = wq.shape[1]
    group = query_cols // head
    q_parts = send_q.shape[0]
    q_width = query_cols // q_parts
    lora_cols = down.shape[1]
    d_bits, r_bits, s_bits = log2(DRAFT), log2(rows), log2(slots)
    rank_bits = log2(ADAPTER_RANK)
    halves = SUB16 // rows
    q_rows = group * DRAFT
    out_rows = tokens // sub
    pieces = SUB16 // out_rows
    o_parts = send_o.shape[0]
    part_cols = wo.shape[1] // o_parts
    piece_cols = part_cols // pieces

    barrier = pltpu.get_barrier_semaphore()
    for o in range(1, feat):
        pl.semaphore_signal(
            barrier, inc=1, device_id={"feat": wrap(me + o, feat)},
            device_id_type=pl.DeviceIdType.MESH,
        )
    for o in range(1, sub):
        pl.semaphore_signal(
            barrier, inc=1, device_id={"sub": wrap(my_sub + o, sub)},
            device_id_type=pl.DeviceIdType.MESH,
        )

    loads = []

    def load(src, dst):
        copy = pltpu.make_async_copy(src, dst, load_sem.at[len(loads)])
        loads.append(copy)
        copy.start()
        return copy

    ld_index = [
        load(owner_hbm, owner_ref), load(adapter_hbm, adapter_ref), load(length_hbm, length_ref)
    ]
    ld_hidden = load(hidden_hbm, hidden)
    ld_gain = load(gain_hbm, gain)
    ld_freq = load(freq_hbm, freq)
    ld_down = load(down_hbm, down)
    ld_wk = load(wk_hbm, wk)
    ld_wv = load(wv_hbm, wv)
    ld_q = [
        load(wq_hbm.at[:, pl.ds(i * q_width, q_width)], wq.at[:, pl.ds(i * q_width, q_width)])
        for i in range(q_parts)
    ]

    for copy in ld_index:
        copy.wait()
    owner = [owner_ref[r, my_sub] for r in range(requests)]
    row_of = []
    for r in range(requests):
        slot = jnp.int32(0)
        for before in range(r):
            slot = slot + jnp.where(owner[before] == owner[r], 1, 0)
        row_of.append(owner[r] * slots + slot)
    adapter = [adapter_ref[r] for r in range(requests)]
    length = [length_ref[r] for r in range(requests)]
    my_adapter, my_length = [], []
    for k in range(slots):
        a, n = jnp.int32(-1), jnp.int32(0)
        for r in range(requests):
            here = row_of[r] == me * slots + k
            a = jnp.where(here, adapter[r], a)
            n = jnp.where(here, length[r], n)
        my_adapter.append(a)
        my_length.append(n)

    def iota(shape, dim):
        return lax.broadcasted_iota(i32, shape, dim)

    def per_request(index, scalars):
        out = jnp.full(index.shape, -1, i32)
        for r in range(requests):
            out = jnp.where(index == r, scalars[r], out)
        return out

    def target_row(j):
        return wrap(me + (j >> r_bits), feat) * slots + ((j >> d_bits) & (slots - 1))

    all_rows = feat * rows
    shape = (all_rows, tokens)
    j, t = iota(shape, 0), iota(shape, 1)
    picked = (per_request(t >> d_bits, row_of) == target_row(j)) & (
        (j & (DRAFT - 1)) == (t & (DRAFT - 1))
    )
    picks = jnp.where(picked, 1.0, 0.0).astype(bf16)

    shape = (all_rows, lora_cols)
    target = target_row(iota(shape, 0))
    row_adapter = jnp.full(shape, -1, i32)
    for r in range(requests):
        row_adapter = jnp.where(target == row_of[r], adapter[r], row_adapter)
    lora_mask = (iota(shape, 1) >> rank_bits) == row_adapter

    def slot_value(shape, scalars):
        index = iota(shape, 0) >> d_bits
        out = jnp.full(shape, scalars[0], i32)
        for k in range(1, slots):
            out = jnp.where(index == k, scalars[k], out)
        return out

    shape = (rows, lora_cols)
    my_lora_mask = (iota(shape, 1) >> rank_bits) == slot_value(shape, my_adapter)

    q_stage[...] = jnp.zeros_like(q_stage)
    ld_hidden.wait()
    ld_gain.wait()
    ld_freq.wait()
    picked_hidden = jnp.dot(picks, hidden[...], preferred_element_type=f32)
    gains = gain[...].astype(f32)
    x = jnp.concatenate(
        [
            picked_hidden[:, i * LANES : (i + 1) * LANES] * gains[i : i + 1, :]
            for i in range(width // LANES)
        ],
        axis=1,
    ).astype(bf16)
    squares = jnp.sum(picked_hidden * picked_hidden, axis=1, keepdims=True)

    shape = (rows, head)
    position = (slot_value(shape, my_length) + (iota(shape, 0) & (DRAFT - 1))).astype(f32)
    angle = position * freq[...]
    cosine = jnp.cos(angle)
    sine = jnp.sin(angle)
    sine = jnp.where(iota(shape, 1) < head // 2, -sine, sine)

    sends = []

    def send(src, dst, ssem, rsem, device):
        copy = pltpu.make_async_remote_copy(
            src_ref=src, dst_ref=dst, send_sem=ssem, recv_sem=rsem,
            device_id=device, device_id_type=pl.DeviceIdType.MESH,
        )
        copy.start()
        sends.append(copy)
        return copy

    ld_wk.wait()
    ld_wv.wait()
    ld_down.wait()
    ld_k = [
        load(keys_hbm.at[s], keys.at[:, pl.ds(s * head, head)]) for s in range(slots)
    ]
    ld_up = load(up_hbm, up)
    part_k = jnp.dot(x, wk[...], preferred_element_type=f32)
    part_v = jnp.dot(x, wv[...], preferred_element_type=f32)
    lora = jnp.where(lora_mask, jnp.dot(x, down[...], preferred_element_type=f32), 0.0)
    folded = lora[:, :LANES]
    for i in range(1, lora_cols // LANES):
        folded = folded + lora[:, i * LANES : (i + 1) * LANES]
    send_a[:, 0:head] = part_k
    send_a[:, head : 2 * head] = part_v
    send_a[:, 2 * head : 2 * head + LANES] = folded
    send_a[:, 2 * head + LANES :] = jnp.broadcast_to(squares, (all_rows, LANES))
    pl.semaphore_wait(barrier, feat + sub - 2)
    first = []
    for o in range(1, feat):
        block = pl.ds(o * rows, rows)
        first.append(
            send(
                send_a.at[block], recv_a.at[block], send_sem.at[0, o], recv_sem.at[0, o],
                {"feat": wrap(me + o, feat)},
            )
        )
    ld_v = []
    for i in range(q_parts):
        ld_q[i].wait()
        if i == 0:
            ld_v = [
                load(values_hbm.at[s], values.at[:, pl.ds(s * head, head)])
                for s in range(slots)
            ]
        if i == q_parts - 1:
            ld_o = [
                load(
                    wo_hbm.at[:, pl.ds(n * part_cols, part_cols)],
                    wo.at[:, pl.ds(n * part_cols, part_cols)],
                )
                for n in range(o_parts)
            ]
        send_q[i] = jnp.dot(
            x, wq[:, i * q_width : (i + 1) * q_width], preferred_element_type=f32
        )
        for o in range(1, feat):
            block = pl.ds(o * rows, rows)
            first.append(
                send(
                    send_q.at[i, block], recv_q.at[i, block],
                    send_sem.at[1 + i, o], recv_sem.at[1 + i, o],
                    {"feat": wrap(me + o, feat)},
                )
            )
    ld_up.wait()
    for copy in first[: feat - 1]:
        copy.wait_recv()
    total_a = send_a[0:rows]
    for o in range(1, feat):
        total_a = total_a + recv_a[o * rows : (o + 1) * rows]
    scale = lax.rsqrt(total_a[:, 2 * head + LANES :] / (width * feat) + norm_eps)
    mid = total_a[:, 2 * head : 2 * head + LANES]
    mid = jnp.where(my_lora_mask, jnp.concatenate([mid] * (lora_cols // LANES), axis=1), 0.0)
    mid1 = mid.astype(bf16).astype(f32)
    rest = mid - mid1
    mid2 = rest.astype(bf16).astype(f32)
    mid3 = rest - mid2
    stacked = jnp.concatenate([mid1, mid2, mid3, jnp.zeros_like(mid)], axis=0).astype(bf16)
    lifted = jnp.dot(stacked, up[...], preferred_element_type=f32)
    lifted = lifted[0:rows] + lifted[rows : 2 * rows] + lifted[2 * rows : 3 * rows]

    def rotate(values_in):
        return values_in * cosine + pltpu.roll(values_in, head // 2, 1) * sine

    key_new = rotate(total_a[:, 0:head] * scale)
    value_new = total_a[:, head : 2 * head] * scale
    filler = jnp.zeros((LANES - rows, head), f32)
    key_new = jnp.concatenate([key_new, filler], axis=0).astype(bf16)
    value_new = jnp.concatenate([value_new, filler], axis=0).astype(bf16)

    for copy in first[feat - 1 :]:
        copy.wait_recv()
    for i in range(q_parts):
        total_q = send_q[i, 0:rows]
        for o in range(1, feat):
            total_q = total_q + recv_q[i, o * rows : (o + 1) * rows]
        for g in range(q_width // head):
            whole_g = i * (q_width // head) + g
            part = total_q[:, g * head : (g + 1) * head]
            part = part + lifted[:, whole_g * head : (whole_g + 1) * head]
            part = rotate(part * scale)
            for s in range(slots):
                at_row = s * q_rows + whole_g * DRAFT
                q_stage[at_row : at_row + DRAFT, s * head : (s + 1) * head] = part[
                    s * DRAFT : (s + 1) * DRAFT
                ]

    for copy in ld_k + ld_v:
        copy.wait()
    factor = head ** (-0.5) * LOG2E
    chunks = context // chunk
    contract = (((1,), (1,)), ((), ()))
    queries = q_stage[...]
    flat = queries[:, 0:head]
    for k in range(1, slots):
        flat = flat + queries[:, k * head : (k + 1) * head]
    queries = queries.astype(bf16)

    def row_slot(shape):
        return iota(shape, 0) >> log2(q_rows)

    shape = (slots * q_rows, LANES)
    draft = iota(shape, 1) - row_slot(shape) * DRAFT
    fresh = lax.dot_general(flat.astype(bf16), key_new, contract, preferred_element_type=f32)
    fresh = jnp.where((draft >= 0) & (draft <= (iota(shape, 0) & (DRAFT - 1))), fresh, -1e30)
    shape = (slots * q_rows, chunk)
    limit = jnp.full(shape, my_length[0], i32)
    for k in range(1, slots):
        limit = jnp.where(row_slot(shape) == k, my_length[k], limit)
    top = fresh
    for c in range(chunks):
        block = lax.dot_general(
            queries, keys[c * chunk : (c + 1) * chunk, :], contract, preferred_element_type=f32
        )
        block = jnp.where(iota(shape, 1) + c * chunk < limit, block, -1e30)
        scores[:, c * chunk : (c + 1) * chunk] = block
        for i in range(chunk // LANES):
            top = jnp.maximum(top, block[:, i * LANES : (i + 1) * LANES])
    row_max = jnp.max(top, axis=1, keepdims=True)
    weights = jnp.exp2((fresh - row_max) * factor)
    total = weights
    summed_new = jnp.dot(weights.astype(bf16), value_new, preferred_element_type=f32)
    summed = jnp.zeros((slots * q_rows, slots * head), f32)
    for c in range(chunks):
        weights = jnp.exp2((scores[:, c * chunk : (c + 1) * chunk] - row_max) * factor)
        for i in range(chunk // LANES):
            total = total + weights[:, i * LANES : (i + 1) * LANES]
        summed = summed + jnp.dot(
            weights.astype(bf16), values[c * chunk : (c + 1) * chunk, :],
            preferred_element_type=f32,
        )
    denominator = jnp.sum(total, axis=1, keepdims=True)
    for s in range(slots):
        span = slice(s * q_rows, (s + 1) * q_rows)
        attended = summed[span, s * head : (s + 1) * head] + summed_new[span]
        attended = attended / denominator[span]
        per_half = group // halves
        for g in range(group):
            h, at = g // per_half, g % per_half
            first_row = h * rows + s * DRAFT
            att_stage[first_row : first_row + DRAFT, at * head : (at + 1) * head] = attended[
                g * DRAFT : (g + 1) * DRAFT
            ]
    att_all[0:SUB16, :] = att_stage[...].astype(bf16)
    second = []
    for o in range(1, feat):
        second.append(
            send(
                att_all.at[pl.ds(0, SUB16)], att_all.at[pl.ds(o * SUB16, SUB16)],
                att_send_sem.at[o], att_recv_sem.at[o], {"feat": wrap(me + o, feat)},
            )
        )
    shape = (tokens, feat * SUB16)
    t, jj = iota(shape, 0), iota(shape, 1)
    out_bits = log2(out_rows)
    token = (wrap(my_sub + (t >> out_bits), sub) << out_bits) + (t & (out_rows - 1))
    source = me - (jj >> log2(SUB16))
    source = jnp.where(source < 0, source + feat, source)
    wanted = source * slots + ((jj >> d_bits) & (slots - 1))
    match = (per_request(token >> d_bits, row_of) == wanted) & (
        (token & (DRAFT - 1)) == (jj & (DRAFT - 1))
    )
    in_half = (jj & (SUB16 - 1)) >> r_bits
    for copy in second:
        copy.wait_recv()
    token_rows = jnp.concatenate(
        [
            jnp.dot(
                jnp.where(match & (in_half == h), 1.0, 0.0).astype(bf16), att_all[...],
                preferred_element_type=f32,
            )
            for h in range(halves)
        ],
        axis=1,
    ).astype(bf16)
    third = []
    for n in range(o_parts):
        ld_o[n].wait()
        block = jnp.dot(
            token_rows, wo[:, n * part_cols : (n + 1) * part_cols], preferred_element_type=f32
        )
        for p in range(pieces):
            for o in range(sub):
                out_stage[n, o, p * out_rows : (p + 1) * out_rows, :] = block[
                    o * out_rows : (o + 1) * out_rows, p * piece_cols : (p + 1) * piece_cols
                ]
        for o in range(1, sub):
            send_o[n, o] = out_stage[n, o].astype(bf16)
            third.append(
                send(
                    send_o.at[n, o], recv_o.at[n, o], out_send_sem.at[n, o],
                    out_recv_sem.at[n, o], {"sub": wrap(my_sub + o, sub)},
                )
            )
    for copy in third:
        copy.wait_recv()
    for n in range(o_parts):
        result = out_stage[n, 0]
        for o in range(1, sub):
            result = result + recv_o[n, o].astype(f32)
        for p in range(pieces):
            first_col = n * part_cols + p * piece_cols
            out_ref[:, first_col : first_col + piece_cols] = result[
                p * out_rows : (p + 1) * out_rows
            ].astype(bf16)
    for copy in sends:
        copy.wait_send()


def body(
    hidden,
    input_norm_gain,
    query_weight,
    key_weight,
    value_weight,
    adapter_down_weight,
    adapter_up_weight,
    output_weight,
    request_adapter,
    stored_owner,
    stored_lengths,
    stored_keys,
    stored_values,
):
    f32, bf16 = jnp.float32, jnp.bfloat16
    feat = lax.axis_size("feat")
    sub = lax.axis_size("sub")
    tokens, width = hidden.shape
    slots, context, head = stored_keys.shape
    rows = slots * DRAFT
    query_cols = query_weight.shape[1]
    out_cols = output_weight.shape[1]
    out_rows = tokens // sub
    q_parts = 2
    o_parts = 2
    chunk = min(2048, context)
    pieces = SUB16 // out_rows
    half = head // 2
    inv_freq = (rope_base ** (-(np.arange(half) * 2.0) / head)).astype(np.float32)
    freq = jnp.asarray(np.tile(np.concatenate([inv_freq, inv_freq])[None, :], (rows, 1)))
    gain = input_norm_gain.reshape(-1, LANES)
    any_spec = pl.BlockSpec(memory_space=pl.ANY)
    V = pltpu.VMEM
    a_cols = 2 * head + 2 * LANES
    scratch = [
        pltpu.SMEM(request_adapter.shape, jnp.int32),
        pltpu.SMEM(stored_owner.shape, jnp.int32),
        pltpu.SMEM(stored_lengths.shape, jnp.int32),
        V(hidden.shape, bf16),
        V(gain.shape, bf16),
        V(freq.shape, f32),
        V(query_weight.shape, bf16),
        V(key_weight.shape, bf16),
        V(value_weight.shape, bf16),
        V(adapter_down_weight.shape, bf16),
        V(adapter_up_weight.shape, bf16),
        V(output_weight.shape, bf16),
        V((context, slots * head), bf16),
        V((context, slots * head), bf16),
        V((feat * rows, a_cols), f32),
        V((feat * rows, a_cols), f32),
        V((q_parts, feat * rows, query_cols // q_parts), f32),
        V((q_parts, feat * rows, query_cols // q_parts), f32),
        V((slots * query_cols // head * DRAFT, slots * head), f32),
        V((slots * query_cols // head * DRAFT, context), f32),
        V((SUB16, query_cols * rows // SUB16), f32),
        V((feat * SUB16, query_cols * rows // SUB16), bf16),
        V((o_parts, sub, SUB16, out_cols // pieces // o_parts), f32),
        V((o_parts, sub, SUB16, out_cols // pieces // o_parts), bf16),
        V((o_parts, sub, SUB16, out_cols // pieces // o_parts), bf16),
        pltpu.SemaphoreType.DMA((11 + o_parts + q_parts + 2 * slots,)),
        pltpu.SemaphoreType.DMA((1 + q_parts, feat)),
        pltpu.SemaphoreType.DMA((1 + q_parts, feat)),
        pltpu.SemaphoreType.DMA((feat,)),
        pltpu.SemaphoreType.DMA((feat,)),
        pltpu.SemaphoreType.DMA((o_parts, sub)),
        pltpu.SemaphoreType.DMA((o_parts, sub)),
    ]
    return pl.pallas_call(
        functools.partial(kernel, feat, sub, chunk),
        out_shape=pltpu.VMEM((out_rows, out_cols), bf16),
        in_specs=[any_spec] * 14,
        out_specs=pl.BlockSpec(memory_space=pltpu.VMEM),
        scratch_shapes=scratch,
        compiler_params=pltpu.CompilerParams(
            collective_id=0, has_side_effects=True, vmem_limit_bytes=63 * 1024 * 1024
        ),
    )(
        request_adapter,
        stored_owner,
        stored_lengths,
        hidden,
        gain,
        freq,
        query_weight,
        key_weight,
        value_weight,
        adapter_down_weight,
        adapter_up_weight,
        output_weight,
        stored_keys,
        stored_values,
    )


def solution(mesh):
    in_specs = (
        P("groups", "feat"),
        P("feat"),
        P("feat", "sub"),
        P("feat", "sub"),
        P("feat", "sub"),
        P("feat", None),
        P(None, "sub"),
        P("sub", "feat"),
        P("groups"),
        P("groups", None),
        P("groups"),
        P(("groups", "feat"), None, "sub"),
        P(("groups", "feat"), None, "sub"),
    )
    out_specs = P(("groups", "sub"), "feat")
    return jax.shard_map(body, mesh=mesh, in_specs=in_specs, out_specs=out_specs, check_vma=False)
```

```python
import functools

import jax
import jax.numpy as jnp
import numpy as np
from jax import lax
from jax.experimental import pallas as pl
from jax.experimental.pallas import tpu as pltpu
from jax.sharding import PartitionSpec as P

ADAPTER_RANK = 64
DRAFT = 4
LANES = 128
SUB16 = 16

norm_eps = 1e-05
rope_base = 500000.0
LOG2E = 1.4426950408889634


def log2(n):
    assert n & (n - 1) == 0
    return n.bit_length() - 1


def wrap(value, n):
    return jnp.where(value >= n, value - n, value)


def kernel(
    feat,
    sub,
    chunk,
    adapter_hbm,
    owner_hbm,
    length_hbm,
    hidden_hbm,
    gain_hbm,
    freq_hbm,
    wq_hbm,
    wk_hbm,
    wv_hbm,
    down_hbm,
    up_hbm,
    wo_hbm,
    keys_hbm,
    values_hbm,
    out_ref,
    adapter_ref,
    owner_ref,
    length_ref,
    hidden,
    gain,
    freq,
    wq,
    wk,
    wv,
    down,
    up,
    wo,
    keys,
    values,
    send_a,
    recv_a,
    send_q,
    recv_q,
    q_stage,
    scores,
    att_stage,
    att_all,
    out_stage,
    send_o,
    recv_o,
    load_sem,
    send_sem,
    recv_sem,
    att_send_sem,
    att_recv_sem,
    out_send_sem,
    out_recv_sem,
):
    f32, bf16, i32 = jnp.float32, jnp.bfloat16, jnp.int32
    me = lax.axis_index("feat")
    my_sub = lax.axis_index("sub")
    tokens, width = hidden.shape
    requests = tokens // DRAFT
    slots, context, head = keys_hbm.shape
    rows = slots * DRAFT
    query_cols = wq.shape[1]
    group = query_cols // head
    q_parts = send_q.shape[0]
    q_width = query_cols // q_parts
    lora_cols = down.shape[1]
    d_bits, r_bits, s_bits = log2(DRAFT), log2(rows), log2(slots)
    rank_bits = log2(ADAPTER_RANK)
    halves = SUB16 // rows
    q_rows = group * DRAFT
    out_rows = tokens // sub
    pieces = SUB16 // out_rows
    o_parts = send_o.shape[0]
    part_cols = wo.shape[1] // o_parts
    piece_cols = part_cols // pieces

    barrier = pltpu.get_barrier_semaphore()
    for o in range(1, feat):
        pl.semaphore_signal(
            barrier, inc=1, device_id={"feat": wrap(me + o, feat)},
            device_id_type=pl.DeviceIdType.MESH,
        )
    for o in range(1, sub):
        pl.semaphore_signal(
            barrier, inc=1, device_id={"sub": wrap(my_sub + o, sub)},
            device_id_type=pl.DeviceIdType.MESH,
        )

    loads = []

    def load(src, dst):
        copy = pltpu.make_async_copy(src, dst, load_sem.at[len(loads)])
        loads.append(copy)
        copy.start()
        return copy

    ld_index = [
        load(owner_hbm, owner_ref), load(adapter_hbm, adapter_ref), load(length_hbm, length_ref)
    ]
    ld_hidden = load(hidden_hbm, hidden)
    ld_gain = load(gain_hbm, gain)
    ld_freq = load(freq_hbm, freq)
    ld_down = load(down_hbm, down)
    ld_wk = load(wk_hbm, wk)
    ld_wv = load(wv_hbm, wv)
    ld_q = [
        load(wq_hbm.at[:, pl.ds(i * q_width, q_width)], wq.at[:, pl.ds(i * q_width, q_width)])
        for i in range(q_parts)
    ]

    for copy in ld_index:
        copy.wait()
    owner = [owner_ref[r, my_sub] for r in range(requests)]
    row_of = []
    for r in range(requests):
        slot = jnp.int32(0)
        for before in range(r):
            slot = slot + jnp.where(owner[before] == owner[r], 1, 0)
        row_of.append(owner[r] * slots + slot)
    adapter = [adapter_ref[r] for r in range(requests)]
    length = [length_ref[r] for r in range(requests)]
    my_adapter, my_length = [], []
    for k in range(slots):
        a, n = jnp.int32(-1), jnp.int32(0)
        for r in range(requests):
            here = row_of[r] == me * slots + k
            a = jnp.where(here, adapter[r], a)
            n = jnp.where(here, length[r], n)
        my_adapter.append(a)
        my_length.append(n)

    def iota(shape, dim):
        return lax.broadcasted_iota(i32, shape, dim)

    def per_request(index, scalars):
        out = jnp.full(index.shape, -1, i32)
        for r in range(requests):
            out = jnp.where(index == r, scalars[r], out)
        return out

    def target_row(j):
        return wrap(me + (j >> r_bits), feat) * slots + ((j >> d_bits) & (slots - 1))

    all_rows = feat * rows
    shape = (all_rows, tokens)
    j, t = iota(shape, 0), iota(shape, 1)
    picked = (per_request(t >> d_bits, row_of) == target_row(j)) & (
        (j & (DRAFT - 1)) == (t & (DRAFT - 1))
    )
    picks = jnp.where(picked, 1.0, 0.0).astype(bf16)

    shape = (all_rows, lora_cols)
    target = target_row(iota(shape, 0))
    row_adapter = jnp.full(shape, -1, i32)
    for r in range(requests):
        row_adapter = jnp.where(target == row_of[r], adapter[r], row_adapter)
    lora_mask = (iota(shape, 1) >> rank_bits) == row_adapter

    def slot_value(shape, scalars):
        index = iota(shape, 0) >> d_bits
        out = jnp.full(shape, scalars[0], i32)
        for k in range(1, slots):
            out = jnp.where(index == k, scalars[k], out)
        return out

    shape = (rows, lora_cols)
    my_lora_mask = (iota(shape, 1) >> rank_bits) == slot_value(shape, my_adapter)

    q_stage[...] = jnp.zeros_like(q_stage)
    ld_hidden.wait()
    ld_gain.wait()
    ld_freq.wait()
    picked_hidden = jnp.dot(picks, hidden[...], preferred_element_type=f32)
    gains = gain[...].astype(f32)
    x = jnp.concatenate(
        [
            picked_hidden[:, i * LANES : (i + 1) * LANES] * gains[i : i + 1, :]
            for i in range(width // LANES)
        ],
        axis=1,
    ).astype(bf16)
    squares = jnp.sum(picked_hidden * picked_hidden, axis=1, keepdims=True)

    shape = (rows, head)
    position = (slot_value(shape, my_length) + (iota(shape, 0) & (DRAFT - 1))).astype(f32)
    angle = position * freq[...]
    cosine = jnp.cos(angle)
    sine = jnp.sin(angle)
    sine = jnp.where(iota(shape, 1) < head // 2, -sine, sine)

    sends = []

    def send(src, dst, ssem, rsem, device):
        copy = pltpu.make_async_remote_copy(
            src_ref=src, dst_ref=dst, send_sem=ssem, recv_sem=rsem,
            device_id=device, device_id_type=pl.DeviceIdType.MESH,
        )
        copy.start()
        sends.append(copy)
        return copy

    ld_wk.wait()
    ld_wv.wait()
    ld_down.wait()
    ld_up = load(up_hbm, up)
    ld_k = [load(keys_hbm.at[s], keys.at[s]) for s in range(slots)]
    part_k = jnp.dot(x, wk[...], preferred_element_type=f32)
    part_v = jnp.dot(x, wv[...], preferred_element_type=f32)
    lora = jnp.where(lora_mask, jnp.dot(x, down[...], preferred_element_type=f32), 0.0)
    folded = lora[:, :LANES]
    for i in range(1, lora_cols // LANES):
        folded = folded + lora[:, i * LANES : (i + 1) * LANES]
    send_a[:, 0:head] = part_k
    send_a[:, head : 2 * head] = part_v
    send_a[:, 2 * head : 2 * head + LANES] = folded
    send_a[:, 2 * head + LANES :] = jnp.broadcast_to(squares, (all_rows, LANES))
    pl.semaphore_wait(barrier, feat + sub - 2)
    first = []
    for o in range(1, feat):
        block = pl.ds(o * rows, rows)
        first.append(
            send(
                send_a.at[block], recv_a.at[block], send_sem.at[0, o], recv_sem.at[0, o],
                {"feat": wrap(me + o, feat)},
            )
        )
    ld_v = []
    for i in range(q_parts):
        ld_q[i].wait()
        if i == 0:
            ld_v = [load(values_hbm.at[s], values.at[s]) for s in range(slots)]
        if i == q_parts - 1:
            ld_o = [
                load(
                    wo_hbm.at[:, pl.ds(n * part_cols, part_cols)],
                    wo.at[:, pl.ds(n * part_cols, part_cols)],
                )
                for n in range(o_parts)
            ]
        send_q[i] = jnp.dot(
            x, wq[:, i * q_width : (i + 1) * q_width], preferred_element_type=f32
        )
        for o in range(1, feat):
            block = pl.ds(o * rows, rows)
            first.append(
                send(
                    send_q.at[i, block], recv_q.at[i, block],
                    send_sem.at[1 + i, o], recv_sem.at[1 + i, o],
                    {"feat": wrap(me + o, feat)},
                )
            )
    ld_up.wait()
    for copy in first[: feat - 1]:
        copy.wait_recv()
    total_a = send_a[0:rows]
    for o in range(1, feat):
        total_a = total_a + recv_a[o * rows : (o + 1) * rows]
    scale = lax.rsqrt(total_a[:, 2 * head + LANES :] / (width * feat) + norm_eps)
    mid = total_a[:, 2 * head : 2 * head + LANES]
    mid = jnp.where(my_lora_mask, jnp.concatenate([mid] * (lora_cols // LANES), axis=1), 0.0)
    mid1 = mid.astype(bf16).astype(f32)
    rest = mid - mid1
    mid2 = rest.astype(bf16).astype(f32)
    mid3 = rest - mid2
    stacked = jnp.concatenate([mid1, mid2, mid3, jnp.zeros_like(mid)], axis=0).astype(bf16)
    lifted = jnp.dot(stacked, up[...], preferred_element_type=f32)
    lifted = lifted[0:rows] + lifted[rows : 2 * rows] + lifted[2 * rows : 3 * rows]

    def rotate(values_in):
        return values_in * cosine + pltpu.roll(values_in, head // 2, 1) * sine

    key_new = rotate(total_a[:, 0:head] * scale)
    value_new = total_a[:, head : 2 * head] * scale
    filler = jnp.zeros((LANES - rows, head), f32)
    key_new = jnp.concatenate([key_new, filler], axis=0).astype(bf16)
    value_new = jnp.concatenate([value_new, filler], axis=0).astype(bf16)

    for copy in first[feat - 1 :]:
        copy.wait_recv()
    for i in range(q_parts):
        total_q = send_q[i, 0:rows]
        for o in range(1, feat):
            total_q = total_q + recv_q[i, o * rows : (o + 1) * rows]
        for g in range(q_width // head):
            whole_g = i * (q_width // head) + g
            part = total_q[:, g * head : (g + 1) * head]
            part = part + lifted[:, whole_g * head : (whole_g + 1) * head]
            part = rotate(part * scale)
            for s in range(slots):
                at_row = s * q_rows + whole_g * DRAFT
                q_stage[at_row : at_row + DRAFT, s * head : (s + 1) * head] = part[
                    s * DRAFT : (s + 1) * DRAFT
                ]

    for copy in ld_k + ld_v:
        copy.wait()
    factor = head ** (-0.5) * LOG2E
    chunks = context // chunk
    contract = (((1,), (1,)), ((), ()))
    queries = q_stage[...]
    flat = queries[:, 0:head]
    for k in range(1, slots):
        flat = flat + queries[:, k * head : (k + 1) * head]
    queries = queries.astype(bf16)

    def row_slot(shape):
        return iota(shape, 0) >> log2(q_rows)

    shape = (slots * q_rows, LANES)
    draft = iota(shape, 1) - row_slot(shape) * DRAFT
    fresh = lax.dot_general(flat.astype(bf16), key_new, contract, preferred_element_type=f32)
    fresh = jnp.where((draft >= 0) & (draft <= (iota(shape, 0) & (DRAFT - 1))), fresh, -1e30)

    def both(ref, c):
        span = slice(c * chunk, (c + 1) * chunk)
        return jnp.concatenate([ref[k, span, :] for k in range(slots)], axis=1)

    tops = [fresh[k * q_rows : (k + 1) * q_rows] for k in range(slots)]
    lane = iota((q_rows, chunk), 1)
    for c in range(chunks):
        block = lax.dot_general(queries, both(keys, c), contract, preferred_element_type=f32)
        for k in range(slots):
            part = block[k * q_rows : (k + 1) * q_rows]
            part = jnp.where(lane < my_length[k] - c * chunk, part, -1e30)
            scores[k * q_rows : (k + 1) * q_rows, c * chunk : (c + 1) * chunk] = part
            for i in range(chunk // LANES):
                tops[k] = jnp.maximum(tops[k], part[:, i * LANES : (i + 1) * LANES])
    row_max = jnp.max(jnp.concatenate(tops, axis=0), axis=1, keepdims=True)
    weights = jnp.exp2((fresh - row_max) * factor)
    total = weights
    summed_new = jnp.dot(weights.astype(bf16), value_new, preferred_element_type=f32)
    summed = jnp.zeros((slots * q_rows, slots * head), f32)
    for c in range(chunks):
        weights = jnp.exp2((scores[:, c * chunk : (c + 1) * chunk] - row_max) * factor)
        for i in range(chunk // LANES):
            total = total + weights[:, i * LANES : (i + 1) * LANES]
        summed = summed + jnp.dot(
            weights.astype(bf16), both(values, c), preferred_element_type=f32
        )
    denominator = jnp.sum(total, axis=1, keepdims=True)
    for s in range(slots):
        span = slice(s * q_rows, (s + 1) * q_rows)
        attended = summed[span, s * head : (s + 1) * head] + summed_new[span]
        attended = attended / denominator[span]
        per_half = group // halves
        for g in range(group):
            h, at = g // per_half, g % per_half
            first_row = h * rows + s * DRAFT
            att_stage[first_row : first_row + DRAFT, at * head : (at + 1) * head] = attended[
                g * DRAFT : (g + 1) * DRAFT
            ]
    att_all[0:SUB16, :] = att_stage[...].astype(bf16)
    second = []
    for o in range(1, feat):
        second.append(
            send(
                att_all.at[pl.ds(0, SUB16)], att_all.at[pl.ds(o * SUB16, SUB16)],
                att_send_sem.at[o], att_recv_sem.at[o], {"feat": wrap(me + o, feat)},
            )
        )
    shape = (tokens, feat * SUB16)
    t, jj = iota(shape, 0), iota(shape, 1)
    out_bits = log2(out_rows)
    token = (wrap(my_sub + (t >> out_bits), sub) << out_bits) + (t & (out_rows - 1))
    source = me - (jj >> log2(SUB16))
    source = jnp.where(source < 0, source + feat, source)
    wanted = source * slots + ((jj >> d_bits) & (slots - 1))
    match = (per_request(token >> d_bits, row_of) == wanted) & (
        (token & (DRAFT - 1)) == (jj & (DRAFT - 1))
    )
    in_half = (jj & (SUB16 - 1)) >> r_bits
    for copy in second:
        copy.wait_recv()
    token_rows = jnp.concatenate(
        [
            jnp.dot(
                jnp.where(match & (in_half == h), 1.0, 0.0).astype(bf16), att_all[...],
                preferred_element_type=f32,
            )
            for h in range(halves)
        ],
        axis=1,
    ).astype(bf16)
    third = []
    for n in range(o_parts):
        ld_o[n].wait()
        block = jnp.dot(
            token_rows, wo[:, n * part_cols : (n + 1) * part_cols], preferred_element_type=f32
        )
        for p in range(pieces):
            for o in range(sub):
                out_stage[n, o, p * out_rows : (p + 1) * out_rows, :] = block[
                    o * out_rows : (o + 1) * out_rows, p * piece_cols : (p + 1) * piece_cols
                ]
        for o in range(1, sub):
            send_o[n, o] = out_stage[n, o].astype(bf16)
            third.append(
                send(
                    send_o.at[n, o], recv_o.at[n, o], out_send_sem.at[n, o],
                    out_recv_sem.at[n, o], {"sub": wrap(my_sub + o, sub)},
                )
            )
    for copy in third:
        copy.wait_recv()
    for n in range(o_parts):
        result = out_stage[n, 0]
        for o in range(1, sub):
            result = result + recv_o[n, o].astype(f32)
        for p in range(pieces):
            first_col = n * part_cols + p * piece_cols
            out_ref[:, first_col : first_col + piece_cols] = result[
                p * out_rows : (p + 1) * out_rows
            ].astype(bf16)
    for copy in sends:
        copy.wait_send()


def body(
    hidden,
    input_norm_gain,
    query_weight,
    key_weight,
    value_weight,
    adapter_down_weight,
    adapter_up_weight,
    output_weight,
    request_adapter,
    stored_owner,
    stored_lengths,
    stored_keys,
    stored_values,
):
    f32, bf16 = jnp.float32, jnp.bfloat16
    feat = lax.axis_size("feat")
    sub = lax.axis_size("sub")
    tokens, width = hidden.shape
    slots, context, head = stored_keys.shape
    rows = slots * DRAFT
    query_cols = query_weight.shape[1]
    out_cols = output_weight.shape[1]
    out_rows = tokens // sub
    q_parts = 2
    o_parts = 2
    chunk = min(512, context)
    pieces = SUB16 // out_rows
    half = head // 2
    inv_freq = (rope_base ** (-(np.arange(half) * 2.0) / head)).astype(np.float32)
    freq = jnp.asarray(np.tile(np.concatenate([inv_freq, inv_freq])[None, :], (rows, 1)))
    gain = input_norm_gain.reshape(-1, LANES)
    any_spec = pl.BlockSpec(memory_space=pl.ANY)
    V = pltpu.VMEM
    a_cols = 2 * head + 2 * LANES
    scratch = [
        pltpu.SMEM(request_adapter.shape, jnp.int32),
        pltpu.SMEM(stored_owner.shape, jnp.int32),
        pltpu.SMEM(stored_lengths.shape, jnp.int32),
        V(hidden.shape, bf16),
        V(gain.shape, bf16),
        V(freq.shape, f32),
        V(query_weight.shape, bf16),
        V(key_weight.shape, bf16),
        V(value_weight.shape, bf16),
        V(adapter_down_weight.shape, bf16),
        V(adapter_up_weight.shape, bf16),
        V(output_weight.shape, bf16),
        V(stored_keys.shape, bf16),
        V(stored_values.shape, bf16),
        V((feat * rows, a_cols), f32),
        V((feat * rows, a_cols), f32),
        V((q_parts, feat * rows, query_cols // q_parts), f32),
        V((q_parts, feat * rows, query_cols // q_parts), f32),
        V((slots * query_cols // head * DRAFT, slots * head), f32),
        V((slots * query_cols // head * DRAFT, context), f32),
        V((SUB16, query_cols * rows // SUB16), f32),
        V((feat * SUB16, query_cols * rows // SUB16), bf16),
        V((o_parts, sub, SUB16, out_cols // pieces // o_parts), f32),
        V((o_parts, sub, SUB16, out_cols // pieces // o_parts), bf16),
        V((o_parts, sub, SUB16, out_cols // pieces // o_parts), bf16),
        pltpu.SemaphoreType.DMA((11 + o_parts + q_parts + 2 * slots,)),
        pltpu.SemaphoreType.DMA((1 + q_parts, feat)),
        pltpu.SemaphoreType.DMA((1 + q_parts, feat)),
        pltpu.SemaphoreType.DMA((feat,)),
        pltpu.SemaphoreType.DMA((feat,)),
        pltpu.SemaphoreType.DMA((o_parts, sub)),
        pltpu.SemaphoreType.DMA((o_parts, sub)),
    ]
    return pl.pallas_call(
        functools.partial(kernel, feat, sub, chunk),
        out_shape=pltpu.VMEM((out_rows, out_cols), bf16),
        in_specs=[any_spec] * 14,
        out_specs=pl.BlockSpec(memory_space=pltpu.VMEM),
        scratch_shapes=scratch,
        compiler_params=pltpu.CompilerParams(
            collective_id=0, has_side_effects=True, vmem_limit_bytes=63 * 1024 * 1024
        ),
    )(
        request_adapter,
        stored_owner,
        stored_lengths,
        hidden,
        gain,
        freq,
        query_weight,
        key_weight,
        value_weight,
        adapter_down_weight,
        adapter_up_weight,
        output_weight,
        stored_keys,
        stored_values,
    )


def solution(mesh):
    in_specs = (
        P("groups", "feat"),
        P("feat"),
        P("feat", "sub"),
        P("feat", "sub"),
        P("feat", "sub"),
        P("feat", None),
        P(None, "sub"),
        P("sub", "feat"),
        P("groups"),
        P("groups", None),
        P("groups"),
        P(("groups", "feat"), None, "sub"),
        P(("groups", "feat"), None, "sub"),
    )
    out_specs = P(("groups", "sub"), "feat")
    return jax.shard_map(body, mesh=mesh, in_specs=in_specs, out_specs=out_specs, check_vma=False)
```

```python
import functools

import jax
import jax.numpy as jnp
import numpy as np
from jax import lax
from jax.experimental import pallas as pl
from jax.experimental.pallas import tpu as pltpu
from jax.sharding import PartitionSpec as P

ADAPTER_RANK = 64
DRAFT = 4
LANES = 128
SUB16 = 16

norm_eps = 1e-05
rope_base = 500000.0
LOG2E = 1.4426950408889634


def log2(n):
    assert n & (n - 1) == 0
    return n.bit_length() - 1


def wrap(value, n):
    return jnp.where(value >= n, value - n, value)


def kernel(
    feat,
    sub,
    chunk,
    block_keys,
    adapter_hbm,
    owner_hbm,
    length_hbm,
    hidden_hbm,
    gain_hbm,
    freq_hbm,
    wq_hbm,
    wk_hbm,
    wv_hbm,
    down_hbm,
    up_hbm,
    wo_hbm,
    keys_hbm,
    values_hbm,
    out_ref,
    adapter_ref,
    owner_ref,
    length_ref,
    hidden,
    gain,
    freq,
    wq,
    wk,
    wv,
    down,
    up,
    wo,
    keys,
    values,
    send_a,
    recv_a,
    send_q,
    recv_q,
    q_stage,
    scores,
    att_stage,
    att_all,
    out_stage,
    send_o,
    recv_o,
    load_sem,
    send_sem,
    recv_sem,
    att_send_sem,
    att_recv_sem,
    out_send_sem,
    out_recv_sem,
):
    f32, bf16, i32 = jnp.float32, jnp.bfloat16, jnp.int32
    me = lax.axis_index("feat")
    my_sub = lax.axis_index("sub")
    tokens, width = hidden.shape
    requests = tokens // DRAFT
    slots, context, head = keys_hbm.shape
    rows = slots * DRAFT
    query_cols = wq.shape[1]
    group = query_cols // head
    q_parts = send_q.shape[0]
    q_width = query_cols // q_parts
    lora_cols = down.shape[1]
    d_bits, r_bits, s_bits = log2(DRAFT), log2(rows), log2(slots)
    rank_bits = log2(ADAPTER_RANK)
    halves = SUB16 // rows
    q_rows = group * DRAFT
    out_rows = tokens // sub
    pieces = SUB16 // out_rows
    o_parts = send_o.shape[0]
    part_cols = wo.shape[1] // o_parts
    piece_cols = part_cols // pieces

    barrier = pltpu.get_barrier_semaphore()
    for o in range(1, feat):
        pl.semaphore_signal(
            barrier, inc=1, device_id={"feat": wrap(me + o, feat)},
            device_id_type=pl.DeviceIdType.MESH,
        )
    for o in range(1, sub):
        pl.semaphore_signal(
            barrier, inc=1, device_id={"sub": wrap(my_sub + o, sub)},
            device_id_type=pl.DeviceIdType.MESH,
        )

    loads = []

    def load(src, dst):
        copy = pltpu.make_async_copy(src, dst, load_sem.at[len(loads)])
        loads.append(copy)
        copy.start()
        return copy

    ld_index = [
        load(owner_hbm, owner_ref), load(adapter_hbm, adapter_ref), load(length_hbm, length_ref)
    ]
    ld_hidden = load(hidden_hbm, hidden)
    ld_gain = load(gain_hbm, gain)
    ld_freq = load(freq_hbm, freq)
    ld_down = load(down_hbm, down)
    ld_wk = load(wk_hbm, wk)
    ld_wv = load(wv_hbm, wv)
    ld_q = [
        load(wq_hbm.at[:, pl.ds(i * q_width, q_width)], wq.at[:, pl.ds(i * q_width, q_width)])
        for i in range(q_parts)
    ]

    for copy in ld_index:
        copy.wait()
    owner = [owner_ref[r, my_sub] for r in range(requests)]
    row_of = []
    for r in range(requests):
        slot = jnp.int32(0)
        for before in range(r):
            slot = slot + jnp.where(owner[before] == owner[r], 1, 0)
        row_of.append(owner[r] * slots + slot)
    adapter = [adapter_ref[r] for r in range(requests)]
    length = [length_ref[r] for r in range(requests)]
    my_adapter, my_length = [], []
    for k in range(slots):
        a, n = jnp.int32(-1), jnp.int32(0)
        for r in range(requests):
            here = row_of[r] == me * slots + k
            a = jnp.where(here, adapter[r], a)
            n = jnp.where(here, length[r], n)
        my_adapter.append(a)
        my_length.append(n)

    def iota(shape, dim):
        return lax.broadcasted_iota(i32, shape, dim)

    def per_request(index, scalars):
        out = jnp.full(index.shape, -1, i32)
        for r in range(requests):
            out = jnp.where(index == r, scalars[r], out)
        return out

    def target_row(j):
        return wrap(me + (j >> r_bits), feat) * slots + ((j >> d_bits) & (slots - 1))

    all_rows = feat * rows
    shape = (all_rows, tokens)
    j, t = iota(shape, 0), iota(shape, 1)
    picked = (per_request(t >> d_bits, row_of) == target_row(j)) & (
        (j & (DRAFT - 1)) == (t & (DRAFT - 1))
    )
    picks = jnp.where(picked, 1.0, 0.0).astype(bf16)

    shape = (all_rows, lora_cols)
    target = target_row(iota(shape, 0))
    row_adapter = jnp.full(shape, -1, i32)
    for r in range(requests):
        row_adapter = jnp.where(target == row_of[r], adapter[r], row_adapter)
    lora_mask = (iota(shape, 1) >> rank_bits) == row_adapter

    def slot_value(shape, scalars):
        index = iota(shape, 0) >> d_bits
        out = jnp.full(shape, scalars[0], i32)
        for k in range(1, slots):
            out = jnp.where(index == k, scalars[k], out)
        return out

    shape = (rows, lora_cols)
    my_lora_mask = (iota(shape, 1) >> rank_bits) == slot_value(shape, my_adapter)

    q_stage[...] = jnp.zeros_like(q_stage)
    ld_hidden.wait()
    ld_gain.wait()
    ld_freq.wait()
    picked_hidden = jnp.dot(picks, hidden[...], preferred_element_type=f32)
    gains = gain[...].astype(f32)
    x = jnp.concatenate(
        [
            picked_hidden[:, i * LANES : (i + 1) * LANES] * gains[i : i + 1, :]
            for i in range(width // LANES)
        ],
        axis=1,
    ).astype(bf16)
    squares = jnp.sum(picked_hidden * picked_hidden, axis=1, keepdims=True)

    shape = (rows, head)
    position = (slot_value(shape, my_length) + (iota(shape, 0) & (DRAFT - 1))).astype(f32)
    angle = position * freq[...]
    cosine = jnp.cos(angle)
    sine = jnp.sin(angle)
    sine = jnp.where(iota(shape, 1) < head // 2, -sine, sine)

    sends = []

    def send(src, dst, ssem, rsem, device):
        copy = pltpu.make_async_remote_copy(
            src_ref=src, dst_ref=dst, send_sem=ssem, recv_sem=rsem,
            device_id=device, device_id_type=pl.DeviceIdType.MESH,
        )
        copy.start()
        sends.append(copy)
        return copy

    ld_wk.wait()
    ld_wv.wait()
    ld_down.wait()
    ld_up = load(up_hbm, up)
    ld_k = [load(keys_hbm.at[s], keys.at[s]) for s in range(slots)]
    part_k = jnp.dot(x, wk[...], preferred_element_type=f32)
    part_v = jnp.dot(x, wv[...], preferred_element_type=f32)
    lora = jnp.where(lora_mask, jnp.dot(x, down[...], preferred_element_type=f32), 0.0)
    folded = lora[:, :LANES]
    for i in range(1, lora_cols // LANES):
        folded = folded + lora[:, i * LANES : (i + 1) * LANES]
    send_a[:, 0:head] = part_k
    send_a[:, head : 2 * head] = part_v
    send_a[:, 2 * head : 2 * head + LANES] = folded
    send_a[:, 2 * head + LANES :] = jnp.broadcast_to(squares, (all_rows, LANES))
    pl.semaphore_wait(barrier, feat + sub - 2)
    first = []
    for o in range(1, feat):
        block = pl.ds(o * rows, rows)
        first.append(
            send(
                send_a.at[block], recv_a.at[block], send_sem.at[0, o], recv_sem.at[0, o],
                {"feat": wrap(me + o, feat)},
            )
        )
    ld_v, own_q = [], []
    for i in range(q_parts):
        ld_q[i].wait()
        if i == 0:
            ld_v = [load(values_hbm.at[s], values.at[s]) for s in range(slots)]
        if i == q_parts - 1:
            ld_o = [
                load(
                    wo_hbm.at[:, pl.ds(n * part_cols, part_cols)],
                    wo.at[:, pl.ds(n * part_cols, part_cols)],
                )
                for n in range(o_parts)
            ]
        part = jnp.dot(x, wq[:, i * q_width : (i + 1) * q_width], preferred_element_type=f32)
        own_q.append(part[0:rows])
        for o in range(1, feat):
            block = part[o * rows : (o + 1) * rows]
            fold = q_width // halves
            block = jnp.concatenate(
                [block[:, h * fold : (h + 1) * fold] for h in range(halves)], axis=0
            )
            send_q[i, o] = block.astype(bf16)
            first.append(
                send(
                    send_q.at[i, o], recv_q.at[i, o], send_sem.at[1 + i, o],
                    recv_sem.at[1 + i, o], {"feat": wrap(me + o, feat)},
                )
            )
    ld_up.wait()
    for copy in first[: feat - 1]:
        copy.wait_recv()
    total_a = send_a[0:rows]
    for o in range(1, feat):
        total_a = total_a + recv_a[o * rows : (o + 1) * rows]
    scale = lax.rsqrt(total_a[:, 2 * head + LANES :] / (width * feat) + norm_eps)
    mid = total_a[:, 2 * head : 2 * head + LANES]
    mid = jnp.where(my_lora_mask, jnp.concatenate([mid] * (lora_cols // LANES), axis=1), 0.0)
    mid1 = mid.astype(bf16).astype(f32)
    rest = mid - mid1
    mid2 = rest.astype(bf16).astype(f32)
    mid3 = rest - mid2
    stacked = jnp.concatenate([mid1, mid2, mid3, jnp.zeros_like(mid)], axis=0).astype(bf16)
    lifted = jnp.dot(stacked, up[...], preferred_element_type=f32)
    lifted = lifted[0:rows] + lifted[rows : 2 * rows] + lifted[2 * rows : 3 * rows]

    def rotate(values_in):
        return values_in * cosine + pltpu.roll(values_in, head // 2, 1) * sine

    key_new = rotate(total_a[:, 0:head] * scale)
    value_new = total_a[:, head : 2 * head] * scale
    filler = jnp.zeros((LANES - rows, head), f32)
    key_new = jnp.concatenate([key_new, filler], axis=0).astype(bf16)
    value_new = jnp.concatenate([value_new, filler], axis=0).astype(bf16)

    for copy in first[feat - 1 :]:
        copy.wait_recv()
    for i in range(q_parts):
        total_q = recv_q[i, 1].astype(f32)
        for o in range(2, feat):
            total_q = total_q + recv_q[i, o].astype(f32)
        total_q = jnp.concatenate(
            [total_q[h * rows : (h + 1) * rows] for h in range(halves)], axis=1
        )
        total_q = total_q + own_q[i]
        for g in range(q_width // head):
            whole_g = i * (q_width // head) + g
            part = total_q[:, g * head : (g + 1) * head]
            part = part + lifted[:, whole_g * head : (whole_g + 1) * head]
            part = rotate(part * scale)
            for s in range(slots):
                at_row = s * q_rows + whole_g * DRAFT
                q_stage[at_row : at_row + DRAFT, s * head : (s + 1) * head] = part[
                    s * DRAFT : (s + 1) * DRAFT
                ]

    for copy in ld_k + ld_v:
        copy.wait()
    factor = head ** (-0.5) * LOG2E
    contract = (((1,), (1,)), ((), ()))
    queries = q_stage[...]
    flat = queries[:, 0:head]
    for k in range(1, slots):
        flat = flat + queries[:, k * head : (k + 1) * head]
    queries = queries.astype(bf16)

    def row_slot(shape):
        return iota(shape, 0) >> log2(q_rows)

    shape = (slots * q_rows, LANES)
    draft = iota(shape, 1) - row_slot(shape) * DRAFT
    fresh = lax.dot_general(flat.astype(bf16), key_new, contract, preferred_element_type=f32)
    fresh = jnp.where((draft >= 0) & (draft <= (iota(shape, 0) & (DRAFT - 1))), fresh, -1e30)

    def both(ref, c):
        span = slice(c * chunk, (c + 1) * chunk)
        return jnp.concatenate([ref[k, span, :] for k in range(slots)], axis=1)

    lane = iota((q_rows, chunk), 1)
    per_block = block_keys // chunk
    blocks = context // block_keys

    def score_block(n):
        tops = [jnp.full((q_rows, LANES), -1e30, f32) for k in range(slots)]
        for c in range(n * per_block, (n + 1) * per_block):
            block = lax.dot_general(queries, both(keys, c), contract, preferred_element_type=f32)
            for k in range(slots):
                part = block[k * q_rows : (k + 1) * q_rows]
                part = jnp.where(lane < my_length[k] - c * chunk, part, -1e30)
                scores[k * q_rows : (k + 1) * q_rows, c * chunk : (c + 1) * chunk] = part
                for i in range(chunk // LANES):
                    tops[k] = jnp.maximum(tops[k], part[:, i * LANES : (i + 1) * LANES])
        return jnp.max(jnp.concatenate(tops, axis=0), axis=1, keepdims=True)

    def weigh_block(n, block_max):
        total, summed = None, None
        for c in range(n * per_block, (n + 1) * per_block):
            weights = jnp.exp2((scores[:, c * chunk : (c + 1) * chunk] - block_max) * factor)
            for i in range(chunk // LANES):
                part = weights[:, i * LANES : (i + 1) * LANES]
                total = part if total is None else total + part
            part = jnp.dot(weights.astype(bf16), both(values, c), preferred_element_type=f32)
            summed = part if summed is None else summed + part
        return total, summed

    maxima, parts = [score_block(0)], []
    for n in range(blocks):
        if n + 1 < blocks:
            maxima.append(score_block(n + 1))
        parts.append(weigh_block(n, maxima[n]))
    row_max = jnp.max(fresh, axis=1, keepdims=True)
    for block_max in maxima:
        row_max = jnp.maximum(row_max, block_max)
    weights = jnp.exp2((fresh - row_max) * factor)
    total = weights
    summed_new = jnp.dot(weights.astype(bf16), value_new, preferred_element_type=f32)
    summed = jnp.zeros((slots * q_rows, slots * head), f32)
    for n in range(blocks):
        shrink = jnp.exp2((maxima[n] - row_max) * factor)
        total = total + parts[n][0] * shrink
        summed = summed + parts[n][1] * shrink
    denominator = jnp.sum(total, axis=1, keepdims=True)
    for s in range(slots):
        span = slice(s * q_rows, (s + 1) * q_rows)
        attended = summed[span, s * head : (s + 1) * head] + summed_new[span]
        attended = attended / denominator[span]
        per_half = group // halves
        for g in range(group):
            h, at = g // per_half, g % per_half
            first_row = h * rows + s * DRAFT
            att_stage[first_row : first_row + DRAFT, at * head : (at + 1) * head] = attended[
                g * DRAFT : (g + 1) * DRAFT
            ]
    att_all[0:SUB16, :] = att_stage[...].astype(bf16)
    second = []
    for o in range(1, feat):
        second.append(
            send(
                att_all.at[pl.ds(0, SUB16)], att_all.at[pl.ds(o * SUB16, SUB16)],
                att_send_sem.at[o], att_recv_sem.at[o], {"feat": wrap(me + o, feat)},
            )
        )
    shape = (tokens, feat * SUB16)
    t, jj = iota(shape, 0), iota(shape, 1)
    out_bits = log2(out_rows)
    token = (wrap(my_sub + (t >> out_bits), sub) << out_bits) + (t & (out_rows - 1))
    source = me - (jj >> log2(SUB16))
    source = jnp.where(source < 0, source + feat, source)
    wanted = source * slots + ((jj >> d_bits) & (slots - 1))
    match = (per_request(token >> d_bits, row_of) == wanted) & (
        (token & (DRAFT - 1)) == (jj & (DRAFT - 1))
    )
    in_half = (jj & (SUB16 - 1)) >> r_bits
    for copy in second:
        copy.wait_recv()
    token_rows = jnp.concatenate(
        [
            jnp.dot(
                jnp.where(match & (in_half == h), 1.0, 0.0).astype(bf16), att_all[...],
                preferred_element_type=f32,
            )
            for h in range(halves)
        ],
        axis=1,
    ).astype(bf16)
    third = []
    for n in range(o_parts):
        ld_o[n].wait()
        block = jnp.dot(
            token_rows, wo[:, n * part_cols : (n + 1) * part_cols], preferred_element_type=f32
        )
        for p in range(pieces):
            for o in range(sub):
                out_stage[n, o, p * out_rows : (p + 1) * out_rows, :] = block[
                    o * out_rows : (o + 1) * out_rows, p * piece_cols : (p + 1) * piece_cols
                ]
        for o in range(1, sub):
            send_o[n, o] = out_stage[n, o].astype(bf16)
            third.append(
                send(
                    send_o.at[n, o], recv_o.at[n, o], out_send_sem.at[n, o],
                    out_recv_sem.at[n, o], {"sub": wrap(my_sub + o, sub)},
                )
            )
    for copy in third:
        copy.wait_recv()
    for n in range(o_parts):
        result = out_stage[n, 0]
        for o in range(1, sub):
            result = result + recv_o[n, o].astype(f32)
        for p in range(pieces):
            first_col = n * part_cols + p * piece_cols
            out_ref[:, first_col : first_col + piece_cols] = result[
                p * out_rows : (p + 1) * out_rows
            ].astype(bf16)
    for copy in sends:
        copy.wait_send()


def body(
    hidden,
    input_norm_gain,
    query_weight,
    key_weight,
    value_weight,
    adapter_down_weight,
    adapter_up_weight,
    output_weight,
    request_adapter,
    stored_owner,
    stored_lengths,
    stored_keys,
    stored_values,
):
    f32, bf16 = jnp.float32, jnp.bfloat16
    feat = lax.axis_size("feat")
    sub = lax.axis_size("sub")
    tokens, width = hidden.shape
    slots, context, head = stored_keys.shape
    rows = slots * DRAFT
    query_cols = query_weight.shape[1]
    out_cols = output_weight.shape[1]
    out_rows = tokens // sub
    q_parts = 2
    o_parts = 2
    chunk = min(512, context)
    block_keys = min(2048, context)
    pieces = SUB16 // out_rows
    half = head // 2
    inv_freq = (rope_base ** (-(np.arange(half) * 2.0) / head)).astype(np.float32)
    freq = jnp.asarray(np.tile(np.concatenate([inv_freq, inv_freq])[None, :], (rows, 1)))
    gain = input_norm_gain.reshape(-1, LANES)
    any_spec = pl.BlockSpec(memory_space=pl.ANY)
    V = pltpu.VMEM
    a_cols = 2 * head + 2 * LANES
    scratch = [
        pltpu.SMEM(request_adapter.shape, jnp.int32),
        pltpu.SMEM(stored_owner.shape, jnp.int32),
        pltpu.SMEM(stored_lengths.shape, jnp.int32),
        V(hidden.shape, bf16),
        V(gain.shape, bf16),
        V(freq.shape, f32),
        V(query_weight.shape, bf16),
        V(key_weight.shape, bf16),
        V(value_weight.shape, bf16),
        V(adapter_down_weight.shape, bf16),
        V(adapter_up_weight.shape, bf16),
        V(output_weight.shape, bf16),
        V(stored_keys.shape, bf16),
        V(stored_values.shape, bf16),
        V((feat * rows, a_cols), f32),
        V((feat * rows, a_cols), f32),
        V((q_parts, feat, SUB16, query_cols // q_parts * rows // SUB16), bf16),
        V((q_parts, feat, SUB16, query_cols // q_parts * rows // SUB16), bf16),
        V((slots * query_cols // head * DRAFT, slots * head), f32),
        V((slots * query_cols // head * DRAFT, context), f32),
        V((SUB16, query_cols * rows // SUB16), f32),
        V((feat * SUB16, query_cols * rows // SUB16), bf16),
        V((o_parts, sub, SUB16, out_cols // pieces // o_parts), f32),
        V((o_parts, sub, SUB16, out_cols // pieces // o_parts), bf16),
        V((o_parts, sub, SUB16, out_cols // pieces // o_parts), bf16),
        pltpu.SemaphoreType.DMA((11 + o_parts + q_parts + 2 * slots,)),
        pltpu.SemaphoreType.DMA((1 + q_parts, feat)),
        pltpu.SemaphoreType.DMA((1 + q_parts, feat)),
        pltpu.SemaphoreType.DMA((feat,)),
        pltpu.SemaphoreType.DMA((feat,)),
        pltpu.SemaphoreType.DMA((o_parts, sub)),
        pltpu.SemaphoreType.DMA((o_parts, sub)),
    ]
    return pl.pallas_call(
        functools.partial(kernel, feat, sub, chunk, block_keys),
        out_shape=pltpu.VMEM((out_rows, out_cols), bf16),
        in_specs=[any_spec] * 14,
        out_specs=pl.BlockSpec(memory_space=pltpu.VMEM),
        scratch_shapes=scratch,
        compiler_params=pltpu.CompilerParams(
            collective_id=0, has_side_effects=True, vmem_limit_bytes=63 * 1024 * 1024
        ),
    )(
        request_adapter,
        stored_owner,
        stored_lengths,
        hidden,
        gain,
        freq,
        query_weight,
        key_weight,
        value_weight,
        adapter_down_weight,
        adapter_up_weight,
        output_weight,
        stored_keys,
        stored_values,
    )


def solution(mesh):
    in_specs = (
        P("groups", "feat"),
        P("feat"),
        P("feat", "sub"),
        P("feat", "sub"),
        P("feat", "sub"),
        P("feat", None),
        P(None, "sub"),
        P("sub", "feat"),
        P("groups"),
        P("groups", None),
        P("groups"),
        P(("groups", "feat"), None, "sub"),
        P(("groups", "feat"), None, "sub"),
    )
    out_specs = P(("groups", "sub"), "feat")
    return jax.shard_map(body, mesh=mesh, in_specs=in_specs, out_specs=out_specs, check_vma=False)
```

```python
import functools

import jax
import jax.numpy as jnp
import numpy as np
from jax import lax
from jax.experimental import pallas as pl
from jax.experimental.pallas import tpu as pltpu
from jax.sharding import PartitionSpec as P

ADAPTER_RANK = 64
DRAFT = 4
LANES = 128
SUB16 = 16

norm_eps = 1e-05
rope_base = 500000.0
LOG2E = 1.4426950408889634


def log2(n):
    assert n & (n - 1) == 0
    return n.bit_length() - 1


def wrap(value, n):
    return jnp.where(value >= n, value - n, value)


def kernel(
    feat,
    sub,
    chunk,
    block_keys,
    adapter_hbm,
    owner_hbm,
    length_hbm,
    hidden_hbm,
    gain_hbm,
    freq_hbm,
    wq_hbm,
    wk_hbm,
    wv_hbm,
    down_hbm,
    up_hbm,
    wo_hbm,
    keys_hbm,
    values_hbm,
    out_ref,
    adapter_ref,
    owner_ref,
    length_ref,
    hidden,
    gain,
    freq,
    wq,
    wk,
    wv,
    down,
    up,
    wo,
    keys,
    values,
    send_a,
    recv_a,
    send_q,
    recv_q,
    q_stage,
    scores,
    att_stage,
    att_all,
    out_stage,
    send_o,
    recv_o,
    load_sem,
    send_sem,
    recv_sem,
    att_send_sem,
    att_recv_sem,
    out_send_sem,
    out_recv_sem,
):
    f32, bf16, i32 = jnp.float32, jnp.bfloat16, jnp.int32
    me = lax.axis_index("feat")
    my_sub = lax.axis_index("sub")
    tokens, width = hidden.shape
    requests = tokens // DRAFT
    slots, context, head = keys_hbm.shape
    rows = slots * DRAFT
    query_cols = wq.shape[1]
    group = query_cols // head
    q_parts = send_q.shape[0]
    q_width = query_cols // q_parts
    lora_cols = down.shape[1]
    d_bits, r_bits, s_bits = log2(DRAFT), log2(rows), log2(slots)
    rank_bits = log2(ADAPTER_RANK)
    halves = SUB16 // rows
    q_rows = group * DRAFT
    out_rows = tokens // sub
    pieces = SUB16 // out_rows
    o_parts = send_o.shape[0]
    part_cols = wo.shape[1] // o_parts
    piece_cols = part_cols // pieces

    barrier = pltpu.get_barrier_semaphore()
    for o in range(1, feat):
        pl.semaphore_signal(
            barrier, inc=1, device_id={"feat": wrap(me + o, feat)},
            device_id_type=pl.DeviceIdType.MESH,
        )
    for o in range(1, sub):
        pl.semaphore_signal(
            barrier, inc=1, device_id={"sub": wrap(my_sub + o, sub)},
            device_id_type=pl.DeviceIdType.MESH,
        )

    loads = []

    def load(src, dst):
        copy = pltpu.make_async_copy(src, dst, load_sem.at[len(loads)])
        loads.append(copy)
        copy.start()
        return copy

    ld_index = [
        load(owner_hbm, owner_ref), load(adapter_hbm, adapter_ref), load(length_hbm, length_ref)
    ]
    ld_hidden = load(hidden_hbm, hidden)
    ld_gain = load(gain_hbm, gain)
    ld_freq = load(freq_hbm, freq)
    ld_down = load(down_hbm, down)
    ld_wk = load(wk_hbm, wk)
    ld_wv = load(wv_hbm, wv)
    ld_q = [
        load(wq_hbm.at[:, pl.ds(i * q_width, q_width)], wq.at[:, pl.ds(i * q_width, q_width)])
        for i in range(q_parts)
    ]

    for copy in ld_index:
        copy.wait()
    owner = [owner_ref[r, my_sub] for r in range(requests)]
    row_of = []
    for r in range(requests):
        slot = jnp.int32(0)
        for before in range(r):
            slot = slot + jnp.where(owner[before] == owner[r], 1, 0)
        row_of.append(owner[r] * slots + slot)
    adapter = [adapter_ref[r] for r in range(requests)]
    length = [length_ref[r] for r in range(requests)]
    my_adapter, my_length = [], []
    for k in range(slots):
        a, n = jnp.int32(-1), jnp.int32(0)
        for r in range(requests):
            here = row_of[r] == me * slots + k
            a = jnp.where(here, adapter[r], a)
            n = jnp.where(here, length[r], n)
        my_adapter.append(a)
        my_length.append(n)

    def iota(shape, dim):
        return lax.broadcasted_iota(i32, shape, dim)

    def per_request(index, scalars):
        out = jnp.full(index.shape, -1, i32)
        for r in range(requests):
            out = jnp.where(index == r, scalars[r], out)
        return out

    def target_row(j):
        return wrap(me + (j >> r_bits), feat) * slots + ((j >> d_bits) & (slots - 1))

    all_rows = feat * rows
    shape = (all_rows, tokens)
    j, t = iota(shape, 0), iota(shape, 1)
    picked = (per_request(t >> d_bits, row_of) == target_row(j)) & (
        (j & (DRAFT - 1)) == (t & (DRAFT - 1))
    )
    picks = jnp.where(picked, 1.0, 0.0).astype(bf16)

    shape = (all_rows, lora_cols)
    target = target_row(iota(shape, 0))
    row_adapter = jnp.full(shape, -1, i32)
    for r in range(requests):
        row_adapter = jnp.where(target == row_of[r], adapter[r], row_adapter)
    lora_mask = (iota(shape, 1) >> rank_bits) == row_adapter

    def slot_value(shape, scalars):
        index = iota(shape, 0) >> d_bits
        out = jnp.full(shape, scalars[0], i32)
        for k in range(1, slots):
            out = jnp.where(index == k, scalars[k], out)
        return out

    shape = (rows, lora_cols)
    my_lora_mask = (iota(shape, 1) >> rank_bits) == slot_value(shape, my_adapter)

    q_stage[...] = jnp.zeros_like(q_stage)
    ld_hidden.wait()
    ld_gain.wait()
    picked_hidden = jnp.dot(picks, hidden[...], preferred_element_type=f32)
    gains = gain[...].astype(f32)
    x = jnp.concatenate(
        [
            picked_hidden[:, i * LANES : (i + 1) * LANES] * gains[i : i + 1, :]
            for i in range(width // LANES)
        ],
        axis=1,
    ).astype(bf16)
    squares = jnp.sum(picked_hidden * picked_hidden, axis=1, keepdims=True)

    sends = []

    def send(src, dst, ssem, rsem, device):
        copy = pltpu.make_async_remote_copy(
            src_ref=src, dst_ref=dst, send_sem=ssem, recv_sem=rsem,
            device_id=device, device_id_type=pl.DeviceIdType.MESH,
        )
        copy.start()
        sends.append(copy)
        return copy

    ld_wk.wait()
    ld_wv.wait()
    ld_down.wait()
    ld_up = load(up_hbm, up)
    ld_k = [load(keys_hbm.at[s], keys.at[s]) for s in range(slots)]
    part_k = jnp.dot(x, wk[...], preferred_element_type=f32)
    part_v = jnp.dot(x, wv[...], preferred_element_type=f32)
    lora = jnp.where(lora_mask, jnp.dot(x, down[...], preferred_element_type=f32), 0.0)
    folded = lora[:, :LANES]
    for i in range(1, lora_cols // LANES):
        folded = folded + lora[:, i * LANES : (i + 1) * LANES]
    send_a[:, 0:head] = part_k
    send_a[:, head : 2 * head] = part_v
    send_a[:, 2 * head : 2 * head + LANES] = folded
    send_a[:, 2 * head + LANES :] = jnp.broadcast_to(squares, (all_rows, LANES))
    pl.semaphore_wait(barrier, feat + sub - 2)
    first = []
    for o in range(1, feat):
        block = pl.ds(o * rows, rows)
        first.append(
            send(
                send_a.at[block], recv_a.at[block], send_sem.at[0, o], recv_sem.at[0, o],
                {"feat": wrap(me + o, feat)},
            )
        )
    ld_v, own_q = [], []
    for i in range(q_parts):
        ld_q[i].wait()
        if i == 0:
            ld_v = [load(values_hbm.at[s], values.at[s]) for s in range(slots)]
        if i == q_parts - 1:
            ld_o = [
                load(
                    wo_hbm.at[:, pl.ds(n * part_cols, part_cols)],
                    wo.at[:, pl.ds(n * part_cols, part_cols)],
                )
                for n in range(o_parts)
            ]
        part = jnp.dot(x, wq[:, i * q_width : (i + 1) * q_width], preferred_element_type=f32)
        own_q.append(part[0:rows])
        for o in range(1, feat):
            block = part[o * rows : (o + 1) * rows]
            fold = q_width // halves
            block = jnp.concatenate(
                [block[:, h * fold : (h + 1) * fold] for h in range(halves)], axis=0
            )
            send_q[i, o] = block.astype(bf16)
            first.append(
                send(
                    send_q.at[i, o], recv_q.at[i, o], send_sem.at[1 + i, o],
                    recv_sem.at[1 + i, o], {"feat": wrap(me + o, feat)},
                )
            )
    ld_freq.wait()
    shape = (rows, head)
    position = (slot_value(shape, my_length) + (iota(shape, 0) & (DRAFT - 1))).astype(f32)
    angle = position * freq[...]
    cosine = jnp.cos(angle)
    sine = jnp.sin(angle)
    sine = jnp.where(iota(shape, 1) < head // 2, -sine, sine)

    ld_up.wait()
    for copy in first[: feat - 1]:
        copy.wait_recv()
    total_a = send_a[0:rows]
    for o in range(1, feat):
        total_a = total_a + recv_a[o * rows : (o + 1) * rows]
    scale = lax.rsqrt(total_a[:, 2 * head + LANES :] / (width * feat) + norm_eps)
    mid = total_a[:, 2 * head : 2 * head + LANES]
    mid = jnp.where(my_lora_mask, jnp.concatenate([mid] * (lora_cols // LANES), axis=1), 0.0)
    mid1 = mid.astype(bf16).astype(f32)
    rest = mid - mid1
    mid2 = rest.astype(bf16).astype(f32)
    mid3 = rest - mid2
    stacked = jnp.concatenate([mid1, mid2, mid3, jnp.zeros_like(mid)], axis=0).astype(bf16)
    lifted = jnp.dot(stacked, up[...], preferred_element_type=f32)
    lifted = lifted[0:rows] + lifted[rows : 2 * rows] + lifted[2 * rows : 3 * rows]

    def rotate(values_in):
        return values_in * cosine + pltpu.roll(values_in, head // 2, 1) * sine

    key_new = rotate(total_a[:, 0:head] * scale)
    value_new = total_a[:, head : 2 * head] * scale
    filler = jnp.zeros((LANES - rows, head), f32)
    key_new = jnp.concatenate([key_new, filler], axis=0).astype(bf16)
    value_new = jnp.concatenate([value_new, filler], axis=0).astype(bf16)

    for copy in first[feat - 1 :]:
        copy.wait_recv()
    for i in range(q_parts):
        total_q = recv_q[i, 1].astype(f32)
        for o in range(2, feat):
            total_q = total_q + recv_q[i, o].astype(f32)
        total_q = jnp.concatenate(
            [total_q[h * rows : (h + 1) * rows] for h in range(halves)], axis=1
        )
        total_q = total_q + own_q[i]
        for g in range(q_width // head):
            whole_g = i * (q_width // head) + g
            part = total_q[:, g * head : (g + 1) * head]
            part = part + lifted[:, whole_g * head : (whole_g + 1) * head]
            part = rotate(part * scale)
            for s in range(slots):
                at_row = s * q_rows + whole_g * DRAFT
                q_stage[at_row : at_row + DRAFT, s * head : (s + 1) * head] = part[
                    s * DRAFT : (s + 1) * DRAFT
                ]

    for copy in ld_k:
        copy.wait()
    factor = head ** (-0.5) * LOG2E
    contract = (((1,), (1,)), ((), ()))
    queries = q_stage[...]
    flat = queries[:, 0:head]
    for k in range(1, slots):
        flat = flat + queries[:, k * head : (k + 1) * head]
    queries = queries.astype(bf16)

    def row_slot(shape):
        return iota(shape, 0) >> log2(q_rows)

    shape = (slots * q_rows, LANES)
    draft = iota(shape, 1) - row_slot(shape) * DRAFT
    fresh = lax.dot_general(flat.astype(bf16), key_new, contract, preferred_element_type=f32)
    fresh = jnp.where((draft >= 0) & (draft <= (iota(shape, 0) & (DRAFT - 1))), fresh, -1e30)

    def both(ref, c):
        span = slice(c * chunk, (c + 1) * chunk)
        return jnp.concatenate([ref[k, span, :] for k in range(slots)], axis=1)

    lane = iota((q_rows, chunk), 1)
    per_block = block_keys // chunk
    blocks = context // block_keys

    def score_block(n):
        tops = [jnp.full((q_rows, LANES), -1e30, f32) for k in range(slots)]
        for c in range(n * per_block, (n + 1) * per_block):
            block = lax.dot_general(queries, both(keys, c), contract, preferred_element_type=f32)
            for k in range(slots):
                part = block[k * q_rows : (k + 1) * q_rows]
                part = jnp.where(lane < my_length[k] - c * chunk, part, -1e30)
                scores[k * q_rows : (k + 1) * q_rows, c * chunk : (c + 1) * chunk] = part
                for i in range(chunk // LANES):
                    tops[k] = jnp.maximum(tops[k], part[:, i * LANES : (i + 1) * LANES])
        return jnp.max(jnp.concatenate(tops, axis=0), axis=1, keepdims=True)

    def weigh_block(n, block_max):
        total, summed = None, None
        for c in range(n * per_block, (n + 1) * per_block):
            weights = jnp.exp2((scores[:, c * chunk : (c + 1) * chunk] - block_max) * factor)
            for i in range(chunk // LANES):
                part = weights[:, i * LANES : (i + 1) * LANES]
                total = part if total is None else total + part
            part = jnp.dot(weights.astype(bf16), both(values, c), preferred_element_type=f32)
            summed = part if summed is None else summed + part
        return total, summed

    maxima, parts = [score_block(0)], []
    for n in range(blocks):
        if n + 1 < blocks:
            maxima.append(score_block(n + 1))
        if n == 0:
            for copy in ld_v:
                copy.wait()
        parts.append(weigh_block(n, maxima[n]))
    row_max = jnp.max(fresh, axis=1, keepdims=True)
    for block_max in maxima:
        row_max = jnp.maximum(row_max, block_max)
    weights = jnp.exp2((fresh - row_max) * factor)
    total = weights
    summed_new = jnp.dot(weights.astype(bf16), value_new, preferred_element_type=f32)
    summed = jnp.zeros((slots * q_rows, slots * head), f32)
    for n in range(blocks):
        shrink = jnp.exp2((maxima[n] - row_max) * factor)
        total = total + parts[n][0] * shrink
        summed = summed + parts[n][1] * shrink
    denominator = jnp.sum(total, axis=1, keepdims=True)
    for s in range(slots):
        span = slice(s * q_rows, (s + 1) * q_rows)
        attended = summed[span, s * head : (s + 1) * head] + summed_new[span]
        attended = attended / denominator[span]
        per_half = group // halves
        for g in range(group):
            h, at = g // per_half, g % per_half
            first_row = h * rows + s * DRAFT
            att_stage[first_row : first_row + DRAFT, at * head : (at + 1) * head] = attended[
                g * DRAFT : (g + 1) * DRAFT
            ]
    att_all[0:SUB16, :] = att_stage[...].astype(bf16)
    second = []
    for o in range(1, feat):
        second.append(
            send(
                att_all.at[pl.ds(0, SUB16)], att_all.at[pl.ds(o * SUB16, SUB16)],
                att_send_sem.at[o], att_recv_sem.at[o], {"feat": wrap(me + o, feat)},
            )
        )
    shape = (tokens, feat * SUB16)
    t, jj = iota(shape, 0), iota(shape, 1)
    out_bits = log2(out_rows)
    token = (wrap(my_sub + (t >> out_bits), sub) << out_bits) + (t & (out_rows - 1))
    source = me - (jj >> log2(SUB16))
    source = jnp.where(source < 0, source + feat, source)
    wanted = source * slots + ((jj >> d_bits) & (slots - 1))
    match = (per_request(token >> d_bits, row_of) == wanted) & (
        (token & (DRAFT - 1)) == (jj & (DRAFT - 1))
    )
    in_half = (jj & (SUB16 - 1)) >> r_bits
    for copy in second:
        copy.wait_recv()
    token_rows = jnp.concatenate(
        [
            jnp.dot(
                jnp.where(match & (in_half == h), 1.0, 0.0).astype(bf16), att_all[...],
                preferred_element_type=f32,
            )
            for h in range(halves)
        ],
        axis=1,
    ).astype(bf16)
    third = []
    for n in range(o_parts):
        ld_o[n].wait()
        block = jnp.dot(
            token_rows, wo[:, n * part_cols : (n + 1) * part_cols], preferred_element_type=f32
        )
        for p in range(pieces):
            for o in range(sub):
                out_stage[n, o, p * out_rows : (p + 1) * out_rows, :] = block[
                    o * out_rows : (o + 1) * out_rows, p * piece_cols : (p + 1) * piece_cols
                ]
        for o in range(1, sub):
            send_o[n, o] = out_stage[n, o].astype(bf16)
            third.append(
                send(
                    send_o.at[n, o], recv_o.at[n, o], out_send_sem.at[n, o],
                    out_recv_sem.at[n, o], {"sub": wrap(my_sub + o, sub)},
                )
            )
    for copy in third:
        copy.wait_recv()
    for n in range(o_parts):
        result = out_stage[n, 0]
        for o in range(1, sub):
            result = result + recv_o[n, o].astype(f32)
        for p in range(pieces):
            first_col = n * part_cols + p * piece_cols
            out_ref[:, first_col : first_col + piece_cols] = result[
                p * out_rows : (p + 1) * out_rows
            ].astype(bf16)
    for copy in sends:
        copy.wait_send()


def body(
    hidden,
    input_norm_gain,
    query_weight,
    key_weight,
    value_weight,
    adapter_down_weight,
    adapter_up_weight,
    output_weight,
    request_adapter,
    stored_owner,
    stored_lengths,
    stored_keys,
    stored_values,
):
    f32, bf16 = jnp.float32, jnp.bfloat16
    feat = lax.axis_size("feat")
    sub = lax.axis_size("sub")
    tokens, width = hidden.shape
    slots, context, head = stored_keys.shape
    rows = slots * DRAFT
    query_cols = query_weight.shape[1]
    out_cols = output_weight.shape[1]
    out_rows = tokens // sub
    q_parts = 2
    o_parts = 2
    chunk = min(512, context)
    block_keys = min(2048, context)
    pieces = SUB16 // out_rows
    half = head // 2
    inv_freq = (rope_base ** (-(np.arange(half) * 2.0) / head)).astype(np.float32)
    freq = jnp.asarray(np.tile(np.concatenate([inv_freq, inv_freq])[None, :], (rows, 1)))
    gain = input_norm_gain.reshape(-1, LANES)
    any_spec = pl.BlockSpec(memory_space=pl.ANY)
    V = pltpu.VMEM
    a_cols = 2 * head + 2 * LANES
    scratch = [
        pltpu.SMEM(request_adapter.shape, jnp.int32),
        pltpu.SMEM(stored_owner.shape, jnp.int32),
        pltpu.SMEM(stored_lengths.shape, jnp.int32),
        V(hidden.shape, bf16),
        V(gain.shape, bf16),
        V(freq.shape, f32),
        V(query_weight.shape, bf16),
        V(key_weight.shape, bf16),
        V(value_weight.shape, bf16),
        V(adapter_down_weight.shape, bf16),
        V(adapter_up_weight.shape, bf16),
        V(output_weight.shape, bf16),
        V(stored_keys.shape, bf16),
        V(stored_values.shape, bf16),
        V((feat * rows, a_cols), f32),
        V((feat * rows, a_cols), f32),
        V((q_parts, feat, SUB16, query_cols // q_parts * rows // SUB16), bf16),
        V((q_parts, feat, SUB16, query_cols // q_parts * rows // SUB16), bf16),
        V((slots * query_cols // head * DRAFT, slots * head), f32),
        V((slots * query_cols // head * DRAFT, context), f32),
        V((SUB16, query_cols * rows // SUB16), f32),
        V((feat * SUB16, query_cols * rows // SUB16), bf16),
        V((o_parts, sub, SUB16, out_cols // pieces // o_parts), f32),
        V((o_parts, sub, SUB16, out_cols // pieces // o_parts), bf16),
        V((o_parts, sub, SUB16, out_cols // pieces // o_parts), bf16),
        pltpu.SemaphoreType.DMA((11 + o_parts + q_parts + 2 * slots,)),
        pltpu.SemaphoreType.DMA((1 + q_parts, feat)),
        pltpu.SemaphoreType.DMA((1 + q_parts, feat)),
        pltpu.SemaphoreType.DMA((feat,)),
        pltpu.SemaphoreType.DMA((feat,)),
        pltpu.SemaphoreType.DMA((o_parts, sub)),
        pltpu.SemaphoreType.DMA((o_parts, sub)),
    ]
    return pl.pallas_call(
        functools.partial(kernel, feat, sub, chunk, block_keys),
        out_shape=pltpu.VMEM((out_rows, out_cols), bf16),
        in_specs=[any_spec] * 14,
        out_specs=pl.BlockSpec(memory_space=pltpu.VMEM),
        scratch_shapes=scratch,
        compiler_params=pltpu.CompilerParams(
            collective_id=0, has_side_effects=True, vmem_limit_bytes=63 * 1024 * 1024
        ),
    )(
        request_adapter,
        stored_owner,
        stored_lengths,
        hidden,
        gain,
        freq,
        query_weight,
        key_weight,
        value_weight,
        adapter_down_weight,
        adapter_up_weight,
        output_weight,
        stored_keys,
        stored_values,
    )


def solution(mesh):
    in_specs = (
        P("groups", "feat"),
        P("feat"),
        P("feat", "sub"),
        P("feat", "sub"),
        P("feat", "sub"),
        P("feat", None),
        P(None, "sub"),
        P("sub", "feat"),
        P("groups"),
        P("groups", None),
        P("groups"),
        P(("groups", "feat"), None, "sub"),
        P(("groups", "feat"), None, "sub"),
    )
    out_specs = P(("groups", "sub"), "feat")
    return jax.shard_map(body, mesh=mesh, in_specs=in_specs, out_specs=out_specs, check_vma=False)
```

```python
import functools

import jax
import jax.numpy as jnp
import numpy as np
from jax import lax
from jax.experimental import pallas as pl
from jax.experimental.pallas import tpu as pltpu
from jax.sharding import PartitionSpec as P

ADAPTER_RANK = 64
DRAFT = 4
LANES = 128
SUB16 = 16

norm_eps = 1e-05
rope_base = 500000.0
LOG2E = 1.4426950408889634


def log2(n):
    assert n & (n - 1) == 0
    return n.bit_length() - 1


def wrap(value, n):
    return jnp.where(value >= n, value - n, value)


def kernel(
    feat,
    sub,
    chunk,
    block_keys,
    adapter_hbm,
    owner_hbm,
    length_hbm,
    hidden_hbm,
    gain_hbm,
    freq_hbm,
    wq_hbm,
    wk_hbm,
    wv_hbm,
    down_hbm,
    up_hbm,
    wo_hbm,
    keys_hbm,
    values_hbm,
    out_ref,
    adapter_ref,
    owner_ref,
    length_ref,
    hidden,
    gain,
    freq,
    wq,
    wk,
    wv,
    down,
    up,
    wo,
    keys,
    values,
    send_a,
    recv_a,
    send_q,
    recv_q,
    q_stage,
    scores,
    att_stage,
    att_all,
    out_stage,
    send_o,
    recv_o,
    load_sem,
    send_sem,
    recv_sem,
    att_send_sem,
    att_recv_sem,
    out_send_sem,
    out_recv_sem,
):
    f32, bf16, i32 = jnp.float32, jnp.bfloat16, jnp.int32
    me = lax.axis_index("feat")
    my_sub = lax.axis_index("sub")
    tokens, width = hidden.shape
    requests = tokens // DRAFT
    slots, context, head = keys_hbm.shape
    rows = slots * DRAFT
    query_cols = wq.shape[1]
    group = query_cols // head
    q_parts = send_q.shape[0]
    q_width = query_cols // q_parts
    lora_cols = down.shape[1]
    d_bits, r_bits, s_bits = log2(DRAFT), log2(rows), log2(slots)
    rank_bits = log2(ADAPTER_RANK)
    halves = SUB16 // rows
    q_rows = group * DRAFT
    out_rows = tokens // sub
    pieces = SUB16 // out_rows
    o_parts = send_o.shape[0]
    part_cols = wo.shape[1] // o_parts
    piece_cols = part_cols // pieces

    barrier = pltpu.get_barrier_semaphore()
    for o in range(1, feat):
        pl.semaphore_signal(
            barrier, inc=1, device_id={"feat": wrap(me + o, feat)},
            device_id_type=pl.DeviceIdType.MESH,
        )
    for o in range(1, sub):
        pl.semaphore_signal(
            barrier, inc=1, device_id={"sub": wrap(my_sub + o, sub)},
            device_id_type=pl.DeviceIdType.MESH,
        )

    loads = []

    def load(src, dst):
        copy = pltpu.make_async_copy(src, dst, load_sem.at[len(loads)])
        loads.append(copy)
        copy.start()
        return copy

    ld_index = [
        load(owner_hbm, owner_ref), load(adapter_hbm, adapter_ref), load(length_hbm, length_ref)
    ]
    ld_hidden = load(hidden_hbm, hidden)
    ld_gain = load(gain_hbm, gain)
    ld_freq = load(freq_hbm, freq)
    ld_down = load(down_hbm, down)
    ld_wk = load(wk_hbm, wk)
    ld_wv = load(wv_hbm, wv)
    ld_q = [
        load(wq_hbm.at[:, pl.ds(i * q_width, q_width)], wq.at[:, pl.ds(i * q_width, q_width)])
        for i in range(q_parts)
    ]

    for copy in ld_index:
        copy.wait()
    owner = [owner_ref[r, my_sub] for r in range(requests)]
    row_of = []
    for r in range(requests):
        slot = jnp.int32(0)
        for before in range(r):
            slot = slot + jnp.where(owner[before] == owner[r], 1, 0)
        row_of.append(owner[r] * slots + slot)
    adapter = [adapter_ref[r] for r in range(requests)]
    length = [length_ref[r] for r in range(requests)]
    my_adapter, my_length = [], []
    for k in range(slots):
        a, n = jnp.int32(-1), jnp.int32(0)
        for r in range(requests):
            here = row_of[r] == me * slots + k
            a = jnp.where(here, adapter[r], a)
            n = jnp.where(here, length[r], n)
        my_adapter.append(a)
        my_length.append(n)

    def iota(shape, dim):
        return lax.broadcasted_iota(i32, shape, dim)

    def per_request(index, scalars):
        out = jnp.full(index.shape, -1, i32)
        for r in range(requests):
            out = jnp.where(index == r, scalars[r], out)
        return out

    def target_row(j):
        return wrap(me + (j >> r_bits), feat) * slots + ((j >> d_bits) & (slots - 1))

    all_rows = feat * rows
    shape = (all_rows, tokens)
    j, t = iota(shape, 0), iota(shape, 1)
    picked = (per_request(t >> d_bits, row_of) == target_row(j)) & (
        (j & (DRAFT - 1)) == (t & (DRAFT - 1))
    )
    picks = jnp.where(picked, 1.0, 0.0).astype(bf16)

    shape = (all_rows, lora_cols)
    target = target_row(iota(shape, 0))
    row_adapter = jnp.full(shape, -1, i32)
    for r in range(requests):
        row_adapter = jnp.where(target == row_of[r], adapter[r], row_adapter)
    lora_mask = (iota(shape, 1) >> rank_bits) == row_adapter

    def slot_value(shape, scalars):
        index = iota(shape, 0) >> d_bits
        out = jnp.full(shape, scalars[0], i32)
        for k in range(1, slots):
            out = jnp.where(index == k, scalars[k], out)
        return out

    shape = (rows, lora_cols)
    my_lora_mask = (iota(shape, 1) >> rank_bits) == slot_value(shape, my_adapter)

    q_stage[...] = jnp.zeros_like(q_stage)
    ld_hidden.wait()
    ld_gain.wait()
    ld_freq.wait()
    picked_hidden = jnp.dot(picks, hidden[...], preferred_element_type=f32)
    gains = gain[...].astype(f32)
    x = jnp.concatenate(
        [
            picked_hidden[:, i * LANES : (i + 1) * LANES] * gains[i : i + 1, :]
            for i in range(width // LANES)
        ],
        axis=1,
    ).astype(bf16)
    squares = jnp.sum(picked_hidden * picked_hidden, axis=1, keepdims=True)

    shape = (rows, head)
    position = (slot_value(shape, my_length) + (iota(shape, 0) & (DRAFT - 1))).astype(f32)
    angle = position * freq[...]
    cosine = jnp.cos(angle)
    sine = jnp.sin(angle)
    sine = jnp.where(iota(shape, 1) < head // 2, -sine, sine)

    sends = []

    def send(src, dst, ssem, rsem, device):
        copy = pltpu.make_async_remote_copy(
            src_ref=src, dst_ref=dst, send_sem=ssem, recv_sem=rsem,
            device_id=device, device_id_type=pl.DeviceIdType.MESH,
        )
        copy.start()
        sends.append(copy)
        return copy

    ld_wk.wait()
    ld_wv.wait()
    ld_down.wait()
    ld_up = load(up_hbm, up)
    ld_k = [load(keys_hbm.at[s], keys.at[s]) for s in range(slots)]
    part_k = jnp.dot(x, wk[...], preferred_element_type=f32)
    part_v = jnp.dot(x, wv[...], preferred_element_type=f32)
    lora = jnp.where(lora_mask, jnp.dot(x, down[...], preferred_element_type=f32), 0.0)
    folded = lora[:, :LANES]
    for i in range(1, lora_cols // LANES):
        folded = folded + lora[:, i * LANES : (i + 1) * LANES]
    send_a[:, 0:head] = part_k
    send_a[:, head : 2 * head] = part_v
    send_a[:, 2 * head : 2 * head + LANES] = folded
    send_a[:, 2 * head + LANES :] = jnp.broadcast_to(squares, (all_rows, LANES))
    pl.semaphore_wait(barrier, feat + sub - 2)
    first = []
    for o in range(1, feat):
        block = pl.ds(o * rows, rows)
        first.append(
            send(
                send_a.at[block], recv_a.at[block], send_sem.at[0, o], recv_sem.at[0, o],
                {"feat": wrap(me + o, feat)},
            )
        )
    ld_v, own_q = [], []
    for i in range(q_parts):
        ld_q[i].wait()
        if i == 0:
            ld_v = [load(values_hbm.at[s], values.at[s]) for s in range(slots)]
        if i == q_parts - 1:
            ld_o = [
                load(
                    wo_hbm.at[:, pl.ds(n * part_cols, part_cols)],
                    wo.at[:, pl.ds(n * part_cols, part_cols)],
                )
                for n in range(o_parts)
            ]
        part = jnp.dot(x, wq[:, i * q_width : (i + 1) * q_width], preferred_element_type=f32)
        own_q.append(part[0:rows])
        for o in range(1, feat):
            block = part[o * rows : (o + 1) * rows]
            fold = q_width // halves
            block = jnp.concatenate(
                [block[:, h * fold : (h + 1) * fold] for h in range(halves)], axis=0
            )
            send_q[i, o] = block.astype(bf16)
            first.append(
                send(
                    send_q.at[i, o], recv_q.at[i, o], send_sem.at[1 + i, o],
                    recv_sem.at[1 + i, o], {"feat": wrap(me + o, feat)},
                )
            )
    ld_up.wait()
    for copy in first[: feat - 1]:
        copy.wait_recv()
    total_a = send_a[0:rows]
    for o in range(1, feat):
        total_a = total_a + recv_a[o * rows : (o + 1) * rows]
    scale = lax.rsqrt(total_a[:, 2 * head + LANES :] / (width * feat) + norm_eps)
    mid = total_a[:, 2 * head : 2 * head + LANES]
    mid = jnp.where(my_lora_mask, jnp.concatenate([mid] * (lora_cols // LANES), axis=1), 0.0)
    mid1 = mid.astype(bf16).astype(f32)
    rest = mid - mid1
    mid2 = rest.astype(bf16).astype(f32)
    mid3 = rest - mid2
    stacked = jnp.concatenate([mid1, mid2, mid3, jnp.zeros_like(mid)], axis=0).astype(bf16)
    lifted = jnp.dot(stacked, up[...], preferred_element_type=f32)
    lifted = lifted[0:rows] + lifted[rows : 2 * rows] + lifted[2 * rows : 3 * rows]

    def rotate(values_in):
        return values_in * cosine + pltpu.roll(values_in, head // 2, 1) * sine

    key_new = rotate(total_a[:, 0:head] * scale)
    value_new = total_a[:, head : 2 * head] * scale
    filler = jnp.zeros((LANES - rows, head), f32)
    key_new = jnp.concatenate([key_new, filler], axis=0).astype(bf16)
    value_new = jnp.concatenate([value_new, filler], axis=0).astype(bf16)

    for copy in first[feat - 1 :]:
        copy.wait_recv()
    for i in range(q_parts):
        total_q = recv_q[i, 1].astype(f32)
        for o in range(2, feat):
            total_q = total_q + recv_q[i, o].astype(f32)
        total_q = jnp.concatenate(
            [total_q[h * rows : (h + 1) * rows] for h in range(halves)], axis=1
        )
        total_q = total_q + own_q[i]
        for g in range(q_width // head):
            whole_g = i * (q_width // head) + g
            part = total_q[:, g * head : (g + 1) * head]
            part = part + lifted[:, whole_g * head : (whole_g + 1) * head]
            part = rotate(part * scale)
            for s in range(slots):
                at_row = s * q_rows + whole_g * DRAFT
                q_stage[at_row : at_row + DRAFT, s * head : (s + 1) * head] = part[
                    s * DRAFT : (s + 1) * DRAFT
                ]

    for copy in ld_k + ld_v:
        copy.wait()
    factor = head ** (-0.5) * LOG2E
    contract = (((1,), (1,)), ((), ()))
    queries = q_stage[...]
    flat = queries[:, 0:head]
    for k in range(1, slots):
        flat = flat + queries[:, k * head : (k + 1) * head]
    queries = queries.astype(bf16)

    def row_slot(shape):
        return iota(shape, 0) >> log2(q_rows)

    shape = (slots * q_rows, LANES)
    draft = iota(shape, 1) - row_slot(shape) * DRAFT
    fresh = lax.dot_general(flat.astype(bf16), key_new, contract, preferred_element_type=f32)
    fresh = jnp.where((draft >= 0) & (draft <= (iota(shape, 0) & (DRAFT - 1))), fresh, -1e30)

    def both(ref, c):
        span = slice(c * chunk, (c + 1) * chunk)
        return jnp.concatenate([ref[k, span, :] for k in range(slots)], axis=1)

    lane = iota((q_rows, chunk), 1)
    per_block = block_keys // chunk
    blocks = context // block_keys

    def score_block(n):
        tops = [jnp.full((q_rows, LANES), -1e30, f32) for k in range(slots)]
        for c in range(n * per_block, (n + 1) * per_block):
            block = lax.dot_general(queries, both(keys, c), contract, preferred_element_type=f32)
            for k in range(slots):
                part = block[k * q_rows : (k + 1) * q_rows]
                part = jnp.where(lane < my_length[k] - c * chunk, part, -1e30)
                scores[k * q_rows : (k + 1) * q_rows, c * chunk : (c + 1) * chunk] = part
                for i in range(chunk // LANES):
                    tops[k] = jnp.maximum(tops[k], part[:, i * LANES : (i + 1) * LANES])
        return jnp.max(jnp.concatenate(tops, axis=0), axis=1, keepdims=True)

    def weigh_block(n, block_max):
        total, summed = None, None
        for c in range(n * per_block, (n + 1) * per_block):
            weights = jnp.exp2((scores[:, c * chunk : (c + 1) * chunk] - block_max) * factor)
            for i in range(chunk // LANES):
                part = weights[:, i * LANES : (i + 1) * LANES]
                total = part if total is None else total + part
            part = jnp.dot(weights.astype(bf16), both(values, c), preferred_element_type=f32)
            summed = part if summed is None else summed + part
        return total, summed

    maxima, parts = [score_block(0)], []
    for n in range(blocks):
        if n + 1 < blocks:
            maxima.append(score_block(n + 1))
        parts.append(weigh_block(n, maxima[n]))
    row_max = jnp.max(fresh, axis=1, keepdims=True)
    for block_max in maxima:
        row_max = jnp.maximum(row_max, block_max)
    weights = jnp.exp2((fresh - row_max) * factor)
    total = weights
    summed_new = jnp.dot(weights.astype(bf16), value_new, preferred_element_type=f32)
    summed = jnp.zeros((slots * q_rows, slots * head), f32)
    for n in range(blocks):
        shrink = jnp.exp2((maxima[n] - row_max) * factor)
        total = total + parts[n][0] * shrink
        summed = summed + parts[n][1] * shrink
    denominator = jnp.sum(total, axis=1, keepdims=True)
    for s in range(slots):
        span = slice(s * q_rows, (s + 1) * q_rows)
        attended = summed[span, s * head : (s + 1) * head] + summed_new[span]
        attended = attended / denominator[span]
        per_half = group // halves
        for g in range(group):
            h, at = g // per_half, g % per_half
            first_row = h * rows + s * DRAFT
            att_stage[first_row : first_row + DRAFT, at * head : (at + 1) * head] = attended[
                g * DRAFT : (g + 1) * DRAFT
            ]
    att_all[0:SUB16, :] = att_stage[...].astype(bf16)
    second = []
    for o in range(1, feat):
        second.append(
            send(
                att_all.at[pl.ds(0, SUB16)], att_all.at[pl.ds(o * SUB16, SUB16)],
                att_send_sem.at[o], att_recv_sem.at[o], {"feat": wrap(me + o, feat)},
            )
        )
    shape = (tokens, feat * SUB16)
    t, jj = iota(shape, 0), iota(shape, 1)
    out_bits = log2(out_rows)
    token = (wrap(my_sub + (t >> out_bits), sub) << out_bits) + (t & (out_rows - 1))
    source = me - (jj >> log2(SUB16))
    source = jnp.where(source < 0, source + feat, source)
    wanted = source * slots + ((jj >> d_bits) & (slots - 1))
    match = (per_request(token >> d_bits, row_of) == wanted) & (
        (token & (DRAFT - 1)) == (jj & (DRAFT - 1))
    )
    in_half = (jj & (SUB16 - 1)) >> r_bits
    for copy in second:
        copy.wait_recv()
    token_rows = jnp.concatenate(
        [
            jnp.dot(
                jnp.where(match & (in_half == h), 1.0, 0.0).astype(bf16), att_all[...],
                preferred_element_type=f32,
            )
            for h in range(halves)
        ],
        axis=1,
    ).astype(bf16)
    third = []
    for n in range(o_parts):
        ld_o[n].wait()
        block = jnp.dot(
            token_rows, wo[:, n * part_cols : (n + 1) * part_cols], preferred_element_type=f32
        )
        for p in range(pieces):
            for o in range(sub):
                out_stage[n, o, p * out_rows : (p + 1) * out_rows, :] = block[
                    o * out_rows : (o + 1) * out_rows, p * piece_cols : (p + 1) * piece_cols
                ]
        for o in range(1, sub):
            send_o[n, o] = out_stage[n, o].astype(bf16)
            third.append(
                send(
                    send_o.at[n, o], recv_o.at[n, o], out_send_sem.at[n, o],
                    out_recv_sem.at[n, o], {"sub": wrap(my_sub + o, sub)},
                )
            )
    for copy in third:
        copy.wait_recv()
    for n in range(o_parts):
        result = out_stage[n, 0]
        for o in range(1, sub):
            result = result + recv_o[n, o].astype(f32)
        for p in range(pieces):
            first_col = n * part_cols + p * piece_cols
            out_ref[:, first_col : first_col + piece_cols] = result[
                p * out_rows : (p + 1) * out_rows
            ].astype(bf16)
    for copy in sends:
        copy.wait_send()


def body(
    hidden,
    input_norm_gain,
    query_weight,
    key_weight,
    value_weight,
    adapter_down_weight,
    adapter_up_weight,
    output_weight,
    request_adapter,
    stored_owner,
    stored_lengths,
    stored_keys,
    stored_values,
):
    f32, bf16 = jnp.float32, jnp.bfloat16
    feat = lax.axis_size("feat")
    sub = lax.axis_size("sub")
    tokens, width = hidden.shape
    slots, context, head = stored_keys.shape
    rows = slots * DRAFT
    query_cols = query_weight.shape[1]
    out_cols = output_weight.shape[1]
    out_rows = tokens // sub
    q_parts = 2
    o_parts = 1
    chunk = min(512, context)
    block_keys = min(2048, context)
    pieces = SUB16 // out_rows
    half = head // 2
    inv_freq = (rope_base ** (-(np.arange(half) * 2.0) / head)).astype(np.float32)
    freq = jnp.asarray(np.tile(np.concatenate([inv_freq, inv_freq])[None, :], (rows, 1)))
    gain = input_norm_gain.reshape(-1, LANES)
    any_spec = pl.BlockSpec(memory_space=pl.ANY)
    V = pltpu.VMEM
    a_cols = 2 * head + 2 * LANES
    scratch = [
        pltpu.SMEM(request_adapter.shape, jnp.int32),
        pltpu.SMEM(stored_owner.shape, jnp.int32),
        pltpu.SMEM(stored_lengths.shape, jnp.int32),
        V(hidden.shape, bf16),
        V(gain.shape, bf16),
        V(freq.shape, f32),
        V(query_weight.shape, bf16),
        V(key_weight.shape, bf16),
        V(value_weight.shape, bf16),
        V(adapter_down_weight.shape, bf16),
        V(adapter_up_weight.shape, bf16),
        V(output_weight.shape, bf16),
        V(stored_keys.shape, bf16),
        V(stored_values.shape, bf16),
        V((feat * rows, a_cols), f32),
        V((feat * rows, a_cols), f32),
        V((q_parts, feat, SUB16, query_cols // q_parts * rows // SUB16), bf16),
        V((q_parts, feat, SUB16, query_cols // q_parts * rows // SUB16), bf16),
        V((slots * query_cols // head * DRAFT, slots * head), f32),
        V((slots * query_cols // head * DRAFT, context), f32),
        V((SUB16, query_cols * rows // SUB16), f32),
        V((feat * SUB16, query_cols * rows // SUB16), bf16),
        V((o_parts, sub, SUB16, out_cols // pieces // o_parts), f32),
        V((o_parts, sub, SUB16, out_cols // pieces // o_parts), bf16),
        V((o_parts, sub, SUB16, out_cols // pieces // o_parts), bf16),
        pltpu.SemaphoreType.DMA((11 + o_parts + q_parts + 2 * slots,)),
        pltpu.SemaphoreType.DMA((1 + q_parts, feat)),
        pltpu.SemaphoreType.DMA((1 + q_parts, feat)),
        pltpu.SemaphoreType.DMA((feat,)),
        pltpu.SemaphoreType.DMA((feat,)),
        pltpu.SemaphoreType.DMA((o_parts, sub)),
        pltpu.SemaphoreType.DMA((o_parts, sub)),
    ]
    return pl.pallas_call(
        functools.partial(kernel, feat, sub, chunk, block_keys),
        out_shape=pltpu.VMEM((out_rows, out_cols), bf16),
        in_specs=[any_spec] * 14,
        out_specs=pl.BlockSpec(memory_space=pltpu.VMEM),
        scratch_shapes=scratch,
        compiler_params=pltpu.CompilerParams(
            collective_id=0, has_side_effects=True, vmem_limit_bytes=63 * 1024 * 1024
        ),
    )(
        request_adapter,
        stored_owner,
        stored_lengths,
        hidden,
        gain,
        freq,
        query_weight,
        key_weight,
        value_weight,
        adapter_down_weight,
        adapter_up_weight,
        output_weight,
        stored_keys,
        stored_values,
    )


def solution(mesh):
    in_specs = (
        P("groups", "feat"),
        P("feat"),
        P("feat", "sub"),
        P("feat", "sub"),
        P("feat", "sub"),
        P("feat", None),
        P(None, "sub"),
        P("sub", "feat"),
        P("groups"),
        P("groups", None),
        P("groups"),
        P(("groups", "feat"), None, "sub"),
        P(("groups", "feat"), None, "sub"),
    )
    out_specs = P(("groups", "sub"), "feat")
    return jax.shard_map(body, mesh=mesh, in_specs=in_specs, out_specs=out_specs, check_vma=False)
```
